256 devices in a mesh: prompt: 8 (over z), group: 8 (over x, core), tensor: 4 (over y).
Axes of the slice: x: 4, y: 4, z: 8, core: 2. Of those that a mesh axis runs over, the one named last changes fastest.
Arguments:
- prompt_q: bfloat16 [8192, 3584], P(('prompt', 'group'), 'tensor'), parts along dimension 0, may hold values from -8 to 8
- prefix_kv: bfloat16 [2, 8192, 512], P(None, ('prompt', 'group', 'tensor')), parts along dimension 1, may hold values from -16 to 16
- resp_q: bfloat16 [16384, 3584], P(('prompt', 'group'), 'tensor'), parts along dimension 0, may hold values from -8 to 8
- resp_kv: bfloat16 [2, 16384, 512], P(None, ('prompt', 'group'), 'tensor'), parts along dimension 1, may hold values from -4 to 4
- resp_segs: int32 [16384], P('prompt'), parts along dimension 0, may hold values from 0 to 31, as said below
- grad_prompt_out: bfloat16 [8192, 3584], P(('prompt', 'group'), 'tensor'), parts along dimension 0, may hold values from -4 to 4
- grad_resp_out: bfloat16 [16384, 3584], P(('prompt', 'group'), 'tensor'), parts along dimension 0, may hold values from -4 to 4
Outputs:
- prompt_out: bfloat16 [8192, 3584], P(('prompt', 'group'), 'tensor'), parts along dimension 0
- resp_out: bfloat16 [16384, 3584], P(('prompt', 'group'), 'tensor'), parts along dimension 0
- grad_prompt_q: bfloat16 [8192, 3584], P(('prompt', 'group'), 'tensor'), parts along dimension 0
- grad_resp_q: bfloat16 [16384, 3584], P(('prompt', 'group'), 'tensor'), parts along dimension 0
- grad_prefix_kv: bfloat16 [2, 8192, 512], P(None, ('prompt', 'group', 'tensor')), parts along dimension 1
- grad_resp_kv: bfloat16 [2, 16384, 512], P(None, ('prompt', 'group'), 'tensor'), parts along dimension 1
The draws below stay inside these ranges and needn't reach their ends.
There are 8 independent parts, one for each index of `prompt`. The reference program is written for one: setup_inputs(seed, part) draws one part's arguments, and reference() takes and returns one part's arrays. A program takes and returns all parts, laid end to end along the dimension named above; each array names one. Nothing has to cross between parts.
Inputs may be any that keep to these rules, and one draw needn't show every extreme that they name: `resp_segs`: row 0 holds 0; the numbers never fall and grow by one where a response starts. A response starts at row 0 and at every row equal to half of 128 plus a multiple of 128; between each two such rows after the first two, and after the last of them, exactly one more response starts. Every response has 1 to 128 rows; the one that starts at half of 128 has exactly 128.
All inputs are finite; a program needn't handle non-finite values.
Results may differ from the reference program's by a relative error of at most 0.02.
Values may be sent and summed in bfloat16 or wider, within the bound.
No kernel may reach another device: no remote copies, remote signals or barrier semaphores. Data moves between devices by JAX's collectives and lax.ppermute only.
A program may use at most 64 MiB of HBM per device.

```python
import jax
import jax.numpy as jnp
from jax import lax

HEADS = 28
KV_HEADS = 4
HEAD_DIM = 128
SEG_MOST = 128
PROMPT = 1024
RESP_ROWS = 2048


def draw_prompt_q(key, part):
    key = jax.random.fold_in(key, 1)
    normal_key = jax.random.fold_in(key, 0)
    entries = jnp.clip(jax.random.normal(normal_key, (PROMPT, HEADS, HEAD_DIM), jnp.float32), -4.0, 4.0)
    return entries.reshape(PROMPT, HEADS * HEAD_DIM).astype(jnp.bfloat16)


def draw_resp_q(key, part):
    key = jax.random.fold_in(key, 3)
    normal_key = jax.random.fold_in(key, 0)
    entries = jnp.clip(jax.random.normal(normal_key, (RESP_ROWS, HEADS, HEAD_DIM), jnp.float32), -4.0, 4.0)
    return entries.reshape(RESP_ROWS, HEADS * HEAD_DIM).astype(jnp.bfloat16)


def draw_prefix_kv(key, part):
    key = jax.random.fold_in(key, 2)
    key_part, value_part = jax.random.split(key, 2)
    key_rows = jnp.clip(jax.random.normal(key_part, (PROMPT, KV_HEADS, HEAD_DIM), jnp.float32), -4.0, 4.0)
    value_rows = jnp.clip(jax.random.normal(value_part, (PROMPT, KV_HEADS, HEAD_DIM), jnp.float32), -4.0, 4.0)
    return jnp.stack((key_rows, value_rows)).reshape(2, PROMPT, KV_HEADS * HEAD_DIM).astype(jnp.bfloat16)


def draw_resp_segs(key, part):
    key = jax.random.fold_in(key, 11)
    stretch_total = RESP_ROWS // SEG_MOST
    half_most = SEG_MOST // 2
    stretch_ids = jnp.arange(1, stretch_total, dtype=jnp.int32)
    room_limit = jnp.where(stretch_ids == stretch_total - 1, half_most, SEG_MOST).astype(jnp.int32)
    inner_offset = jax.random.randint(key, (stretch_total - 1,), 1, room_limit).astype(jnp.int32)
    extra_rows = (half_most + SEG_MOST * stretch_ids + inner_offset).astype(jnp.int32)
    positions = jnp.arange(RESP_ROWS, dtype=jnp.int32)
    required = positions % SEG_MOST == half_most
    extra_start = jnp.any(positions[:, None] == extra_rows[None, :], axis=1)
    starts = required | extra_start | (positions == 0)
    return (jnp.cumsum(starts.astype(jnp.int32)) - 1).astype(jnp.int32)


def steps_of(own_key, shape, shards, least, top_value):
    def one(dim, parts):
        steps = jax.random.uniform(jax.random.fold_in(jax.random.fold_in(own_key, 6), dim), (parts,), jnp.float32, least / len(shards), top_value / len(shards))
        return jnp.repeat(jnp.exp(steps), shape[dim] // parts).reshape((-1,) + (1,) * (len(shape) - dim - 1))

    gain = one(*shards[0])
    for cut in shards[1:]:
        gain = gain * one(*cut)
    return gain


def scatter_about(key, extent, width, reach, cuts=(), kind=jnp.bfloat16):
    array = width * jax.random.normal(key, extent, jnp.float32)
    if cuts:
        array = array * steps_of(key, extent, cuts, -0.22, 0.18)
    return jnp.clip(array, -reach, reach).astype(kind)


def setup_inputs(seed: int = 0, part: int = 0) -> dict:
    seeds = jax.random.split(jax.random.key(seed), 8)
    own_keys = jax.random.split(jax.random.fold_in(seeds[7], part), 8)
    return {
        "prompt_q": draw_prompt_q(jax.random.fold_in(jax.random.fold_in(seeds[7], part), 71), part),
        "prefix_kv": draw_prefix_kv(jax.random.fold_in(jax.random.fold_in(seeds[7], part), 71), part),
        "resp_q": draw_resp_q(jax.random.fold_in(jax.random.fold_in(seeds[7], part), 71), part),
        "resp_kv": scatter_about(own_keys[3], (2, RESP_ROWS, KV_HEADS * HEAD_DIM), 1.0, 4.0, ((1, 8), (2, 4))),
        "resp_segs": draw_resp_segs(jax.random.fold_in(jax.random.fold_in(seeds[7], part), 71), part),
        "grad_prompt_out": scatter_about(own_keys[5], (PROMPT, HEADS * HEAD_DIM), 1.0, 4.0, ((0, 8), (1, 4))),
        "grad_resp_out": scatter_about(own_keys[6], (RESP_ROWS, HEADS * HEAD_DIM), 1.0, 4.0, ((0, 8), (1, 4))),
    }


def head_pass(queries, upstream, key_rows, value_rows, visible):
    score_scale = HEAD_DIM ** -0.5
    scores = jnp.dot(queries, key_rows.T, preferred_element_type=jnp.float32) * score_scale
    scores = jnp.where(visible, scores, -jnp.inf)
    row_peak = jnp.max(scores, axis=1, keepdims=True)
    raised = jnp.exp(scores - row_peak)
    weights = (raised / jnp.sum(raised, axis=1, keepdims=True)).astype(jnp.bfloat16)
    outputs = jnp.dot(weights, value_rows, preferred_element_type=jnp.float32).astype(jnp.bfloat16)
    row_delta = jnp.sum(upstream.astype(jnp.float32) * outputs.astype(jnp.float32), axis=1, keepdims=True)
    grad_prob = jnp.dot(upstream, value_rows.T, preferred_element_type=jnp.float32)
    dscore = (weights.astype(jnp.float32) * (grad_prob - row_delta)).astype(jnp.bfloat16)
    grad_query = (jnp.dot(dscore, key_rows, preferred_element_type=jnp.float32) * score_scale).astype(jnp.bfloat16)
    grad_key = jnp.dot(dscore.T, queries, preferred_element_type=jnp.float32) * score_scale
    grad_value = jnp.dot(weights.T, upstream, preferred_element_type=jnp.float32)
    return outputs, grad_query, grad_key, grad_value


def reference(prompt_q, prefix_kv, resp_q, resp_kv, resp_segs, grad_prompt_out, grad_resp_out):
    group_heads = HEADS // KV_HEADS
    all_rows = PROMPT + RESP_ROWS
    queries = jnp.concatenate([prompt_q, resp_q], axis=0).reshape(all_rows, HEADS, HEAD_DIM).transpose(1, 0, 2)
    upstream = jnp.concatenate([grad_prompt_out, grad_resp_out], axis=0).reshape(all_rows, HEADS, HEAD_DIM).transpose(1, 0, 2)
    key_rows = jnp.concatenate([prefix_kv[0], resp_kv[0]], axis=0).reshape(all_rows, KV_HEADS, HEAD_DIM).transpose(1, 0, 2)
    value_rows = jnp.concatenate([prefix_kv[1], resp_kv[1]], axis=0).reshape(all_rows, KV_HEADS, HEAD_DIM).transpose(1, 0, 2)
    seg_all = jnp.concatenate([jnp.full((PROMPT,), -1, jnp.int32), resp_segs.astype(jnp.int32)])
    position = jnp.arange(all_rows, dtype=jnp.int32)
    visible = (position[None, :] <= position[:, None]) & ((position[None, :] < PROMPT) | (seg_all[None, :] == seg_all[:, None]))

    def one_head(head_index):
        shared = head_index // group_heads
        return head_pass(queries[head_index], upstream[head_index], key_rows[shared], value_rows[shared], visible)

    outputs, grad_query, grad_key, grad_value = lax.map(one_head, jnp.arange(HEADS, dtype=jnp.int32))
    grad_key = grad_key.reshape(KV_HEADS, group_heads, all_rows, HEAD_DIM).sum(axis=1)
    grad_value = grad_value.reshape(KV_HEADS, group_heads, all_rows, HEAD_DIM).sum(axis=1)
    flat_out = outputs.transpose(1, 0, 2).reshape(all_rows, HEADS * HEAD_DIM)
    flat_grad = grad_query.transpose(1, 0, 2).reshape(all_rows, HEADS * HEAD_DIM)
    kv_grads = jnp.stack([grad_key, grad_value]).transpose(0, 2, 1, 3).reshape(2, all_rows, KV_HEADS * HEAD_DIM).astype(jnp.bfloat16)
    return (flat_out[:PROMPT], flat_out[PROMPT:], flat_grad[:PROMPT], flat_grad[PROMPT:], kv_grads[:, :PROMPT], kv_grads[:, PROMPT:])
```

```python
import functools
import math

import jax
import jax.numpy as jnp
from jax import lax
from jax.experimental import pallas as pl
from jax.experimental.pallas import tpu as pltpu
from jax.sharding import PartitionSpec as P

D = 128
BF = jnp.bfloat16
F = jnp.float32
SCALE = D**-0.5
SCALE2 = SCALE * math.log2(math.e)
MASKED = -1e30
BACK = 64
NT = (((1,), (1,)), ((), ()))
TN = (((0,), (0,)), ((), ()))
NN = (((1,), (0,)), ((), ()))
BLOCK = 256


def mm(a, b, dims):
    return lax.dot_general(a, b, dims, preferred_element_type=F)


def attend(
    kv_ref, lkv_ref, bias_p_ref, bias_l_ref, qr_ref, gr_ref, qp_ref, gp_ref,
    or_ref, op_ref, dqr_ref, dqp_ref, dkv_ref, dlkv_ref,
    k_s, v_s, s_s, w_s, accp, accl, *, heads,
):
    h = pl.program_id(0)
    keys = k_s.shape[0]
    parts = dkv_ref.shape[0]

    @pl.when(h == 0)
    def _():
        k_s[...] = kv_ref[:, 0].reshape(keys, D)
        v_s[...] = kv_ref[:, 1].reshape(keys, D)
        accp[...] = jnp.zeros_like(accp)
        accl[...] = jnp.zeros_like(accl)

    q = jnp.concatenate([qr_ref[...], qp_ref[...]], 0)
    g = jnp.concatenate([gr_ref[...], gp_ref[...]], 0)
    lk = lkv_ref[0]
    lv = lkv_ref[1]
    blocks = [pl.ds(j, BLOCK) for j in range(0, keys, BLOCK)]
    m = None
    for sl in blocks:
        s = mm(k_s[sl, :], q, NT)
        sr = s[:, :256]
        sp = s[:, 256:] + bias_p_ref[sl, :]
        s_s[sl, :256] = sr
        s_s[sl, 256:] = sp
        mj = jnp.concatenate(
            [jnp.max(sr.reshape(BLOCK // 8, 8, 256), 0), jnp.max(sp.reshape(BLOCK // 8, 8, 128), 0)], 1
        )
        m = mj if m is None else jnp.maximum(m, mj)
    sa = mm(lk[0:192], q[0:128], NT) + bias_l_ref[0]
    sb = mm(lk[128:320], q[128:256], NT) + bias_l_ref[1]
    m = jnp.max(m, 0, keepdims=True)
    ma = jnp.maximum(m[:, :128], jnp.max(sa, 0, keepdims=True))
    mb = jnp.maximum(m[:, 128:256], jnp.max(sb, 0, keepdims=True))
    mc = jnp.concatenate([ma, mb, m[:, 256:]], 1) * SCALE2
    pa = jnp.exp2(sa * SCALE2 - mc[:, :128])
    pb = jnp.exp2(sb * SCALE2 - mc[:, 128:256])
    total = None
    for sl in blocks:
        p = jnp.exp2(s_s[sl, :] * SCALE2 - mc)
        s_s[sl, :] = p
        tj = jnp.sum(p.reshape(BLOCK // 8, 8, 384), 0)
        total = tj if total is None else total + tj
    total = jnp.sum(total, 0, keepdims=True)
    ta = total[:, :128] + jnp.sum(pa, 0, keepdims=True)
    tb = total[:, 128:256] + jnp.sum(pb, 0, keepdims=True)
    inv = 1.0 / jnp.concatenate([ta, tb, total[:, 256:]], 1)
    wa = (pa * inv[:, :128]).astype(BF)
    wb = (pb * inv[:, 128:256]).astype(BF)
    o = jnp.zeros((384, D), F)
    for sl in blocks:
        w = (s_s[sl, :] * inv).astype(BF)
        w_s[sl, :] = w
        o = o + mm(w, v_s[sl, :], TN)
        accp[1, sl, :] += mm(w, g, NN)
    oa = mm(wa, lv[0:192], TN)
    ob = mm(wb, lv[128:320], TN)
    o = jnp.concatenate([o[:128] + oa, o[128:256] + ob, o[256:]], 0).astype(BF)
    or_ref[...] = o[:256]
    op_ref[...] = o[256:]
    delta = jnp.sum((g.astype(F) * o.astype(F)).T, 0, keepdims=True)
    accl[1, 0:192, :] += mm(wa, g[:128], NN)
    accl[1, 128:320, :] += mm(wb, g[128:256], NN)
    dq = jnp.zeros((384, D), F)
    for sl in blocks:
        dp = mm(v_s[sl, :], g, NT)
        ds = (w_s[sl, :].astype(F) * (dp - delta)).astype(BF)
        dq = dq + mm(ds, k_s[sl, :], TN)
        accp[0, sl, :] += mm(ds, q, NN)
    dsa = (wa.astype(F) * (mm(lv[0:192], g[:128], NT) - delta[:, :128])).astype(BF)
    dsb = (wb.astype(F) * (mm(lv[128:320], g[128:256], NT) - delta[:, 128:256])).astype(BF)
    dqa = mm(dsa, lk[0:192], TN)
    dqb = mm(dsb, lk[128:320], TN)
    accl[0, 0:192, :] += mm(dsa, q[:128], NN)
    accl[0, 128:320, :] += mm(dsb, q[128:256], NN)
    dqr_ref[...] = (jnp.concatenate([dq[:128] + dqa, dq[128:256] + dqb], 0) * SCALE).astype(BF)
    dqp_ref[...] = (dq[256:] * SCALE).astype(BF)

    @pl.when(h == heads - 1)
    def _():
        dkv_ref[:, 0] = (accp[0] * SCALE).astype(BF).reshape(parts, keys // parts, D)
        dkv_ref[:, 1] = accp[1].astype(BF).reshape(parts, keys // parts, D)
        dlkv_ref[0] = accl[0] * SCALE
        dlkv_ref[1] = accl[1]


def attention(kv, lkv, bias_p, bias_l, qr, gr, qp, gp):
    heads = qr.shape[1] // D
    keys = kv.shape[0] * kv.shape[2]
    whole = lambda a: pl.BlockSpec(a.shape, lambda h: (0,) * len(a.shape))
    head = lambda n: pl.BlockSpec((n, D), lambda h: (0, h))
    shape = jax.ShapeDtypeStruct
    outs = [shape(qr.shape, BF), shape(qp.shape, BF), shape(qr.shape, BF), shape(qp.shape, BF)]
    outs += [shape(kv.shape, BF), shape(lkv.shape, F)]
    pairs = keys * 384 * heads
    return pl.pallas_call(
        functools.partial(attend, heads=heads),
        grid=(heads,),
        in_specs=[whole(kv), whole(lkv), whole(bias_p), whole(bias_l), head(256), head(256), head(128), head(128)],
        out_specs=[head(256), head(128), head(256), head(128), whole(outs[4]), whole(outs[5])],
        out_shape=outs,
        scratch_shapes=[
            pltpu.VMEM((keys, D), BF),
            pltpu.VMEM((keys, D), BF),
            pltpu.VMEM((keys, 384), F),
            pltpu.VMEM((keys, 384), BF),
            pltpu.VMEM((2, keys, D), F),
            pltpu.VMEM((2, 320, D), F),
        ],
        compiler_params=pltpu.CompilerParams(vmem_limit_bytes=48 * 2**20),
        cost_estimate=pl.CostEstimate(flops=pairs * 1280, bytes_accessed=4 * 2**20, transcendentals=pairs),
        name="attend",
    )(kv, lkv, bias_p, bias_l, qr, gr, qp, gp)


def local(prompt_q, prefix_kv, resp_q, resp_kv, resp_segs, grad_prompt_out, grad_resp_out):
    groups = lax.axis_size("group")
    tensors = lax.axis_size("tensor")
    group_rank = lax.axis_index("group")
    rows = prefix_kv.shape[1]
    resp_dev = resp_q.shape[0]
    prompt_dev = prompt_q.shape[0]
    keys = rows * groups * tensors
    both = ("group", "tensor")

    by_head = prefix_kv.reshape(2, rows, tensors, D).transpose(2, 0, 1, 3)
    to_send = jnp.broadcast_to(by_head[None], (groups,) + by_head.shape).reshape(-1, 2, rows, D)
    kv = lax.all_to_all(to_send, both, 0, 0, tiled=True)
    prior = lax.ppermute(
        resp_kv[:, resp_dev - BACK :], "group", [(i, i + 1) for i in range(groups - 1)]
    )
    lkv = jnp.concatenate([prior, resp_kv], 1)

    segs = jnp.concatenate([jnp.full((BACK,), -1, jnp.int32), resp_segs])
    segs = lax.dynamic_slice_in_dim(segs, group_rank * resp_dev, BACK + resp_dev)
    places = jnp.arange(BACK + resp_dev, dtype=jnp.int32)

    def local_bias(k0, k1, q0, q1):
        same = segs[k0:k1, None] == segs[None, q0:q1]
        return jnp.where(same & (places[k0:k1, None] <= places[None, q0:q1]), 0.0, MASKED).astype(F)

    bias_l = jnp.stack([local_bias(0, 192, 64, 192), local_bias(128, 320, 192, 320)])
    query_rows = group_rank * prompt_dev + jnp.arange(prompt_dev, dtype=jnp.int32)
    bias_p = jnp.where(
        jnp.arange(keys, dtype=jnp.int32)[:, None] <= query_rows[None, :], 0.0, MASKED
    ).astype(F)

    resp_out, prompt_out, grad_resp_q, grad_prompt_q, terms, local_terms = attention(
        kv, lkv, bias_p, bias_l, resp_q, grad_resp_out, prompt_q, grad_prompt_out
    )
    arrived = lax.all_to_all(terms, both, 0, 0, tiled=True)
    later = lax.ppermute(
        local_terms[:, :BACK].astype(BF), "group", [(i, i - 1) for i in range(1, groups)]
    )
    grad_resp_kv = jnp.concatenate(
        [local_terms[:, BACK:resp_dev], local_terms[:, resp_dev:] + later.astype(F)], 1
    ).astype(BF)
    summed = arrived.reshape(groups, tensors, 2, rows, D).astype(F).sum(0).astype(BF)
    grad_prefix_kv = summed.transpose(1, 2, 0, 3).reshape(2, rows, tensors * D)
    return (prompt_out, resp_out, grad_prompt_q, grad_resp_q, grad_prefix_kv, grad_resp_kv)


def solution(mesh):
    wide = P(("prompt", "group"), "tensor")
    cache = P(None, ("prompt", "group", "tensor"), None)
    packed = P(None, ("prompt", "group"), "tensor")
    return jax.shard_map(
        local,
        mesh=mesh,
        in_specs=(wide, cache, wide, packed, P("prompt"), wide, wide),
        out_specs=(wide, wide, wide, wide, cache, packed),
        check_vma=False,
    )
```

```python
import math

import jax
import jax.numpy as jnp
from jax import lax
from jax.experimental import pallas as pl
from jax.experimental.pallas import tpu as pltpu
from jax.sharding import PartitionSpec as P

D = 128
BF = jnp.bfloat16
F = jnp.float32
SCALE = D**-0.5
SCALE2 = SCALE * math.log2(math.e)
MASKED = -1e30
BACK = 64
NT = (((1,), (1,)), ((), ()))
TN = (((0,), (0,)), ((), ()))
NN = (((1,), (0,)), ((), ()))
CHUNK = 512


def mm(a, b, dims):
    return lax.dot_general(a, b, dims, preferred_element_type=F)


def fold(x, op):
    return op(x.reshape(x.shape[0] // 8, 8, x.shape[1]), 0)


def stack_heads(ref, rows):
    return jnp.concatenate([ref[rows, i : i + D] for i in range(0, ref.shape[1], D)], 0)


def halves(resp):
    half = resp // 2
    return [(i, slice(i * half, (i + 1) * half), slice(i * half, i * half + half + BACK)) for i in range(2)]


def local_forward(lkv_ref, bias_ref, q_ref, g_ref, p_ref, stat_ref):
    heads = q_ref.shape[1] // D
    for i, rows, keys in halves(q_ref.shape[0]):
        q = stack_heads(q_ref, rows)
        g = stack_heads(g_ref, rows)
        s = mm(lkv_ref[0, keys], q, NT) + jnp.concatenate([bias_ref[i]] * heads, 1)
        m = jnp.max(s, 0, keepdims=True)
        p = jnp.exp2((s - m) * SCALE2)
        dp = mm(lkv_ref[1, keys], g, NT)
        p_ref[i] = p.astype(BF)
        total = jnp.sum(p, 0, keepdims=True)
        mix = jnp.sum(p * dp, 0, keepdims=True)
        for h in range(heads):
            c = slice(h * 128, (h + 1) * 128)
            stat_ref[h, 0:1, rows] = m[:, c]
            stat_ref[h, 1:2, rows] = total[:, c]
            stat_ref[h, 2:3, rows] = mix[:, c]


def local_backward(lkv_ref, p_ref, fs_ref, q_ref, g_ref, o1_ref, dq1_ref, dlkv_ref, o_ref, dq_ref):
    heads = q_ref.shape[1] // D
    terms = []
    for i, rows, keys in halves(q_ref.shape[0]):
        q = stack_heads(q_ref, rows)
        g = stack_heads(g_ref, rows)
        f = jnp.concatenate([fs_ref[h, 0:1, rows] for h in range(heads)], 1)
        delta = jnp.concatenate([fs_ref[h, 1:2, rows] for h in range(heads)], 1)
        k = lkv_ref[0, keys]
        v = lkv_ref[1, keys]
        wf = p_ref[i].astype(F) * f
        w = wf.astype(BF)
        ds = (wf * (mm(v, g, NT) - delta)).astype(BF)
        terms.append((mm(ds, q, NN) * SCALE, mm(w, g, NN)))
        o = mm(w, v, TN)
        dq = mm(ds, k, TN) * SCALE
        for h in range(heads):
            c = slice(h * D, (h + 1) * D)
            r = slice(h * 128, (h + 1) * 128)
            o_ref[rows, c] = (o[r] + o1_ref[rows, c]).astype(BF)
            dq_ref[rows, c] = (dq[r] + dq1_ref[rows, c]).astype(BF)
    for x in range(2):
        a, b = terms[0][x], terms[1][x]
        dlkv_ref[x, 0:128] = a[0:128]
        dlkv_ref[x, 128:192] = a[128:192] + b[0:64]
        dlkv_ref[x, 192:320] = b[64:192]


def prefix_attention(
    first_ref, kv_ref, stat_ref, qr_ref, gr_ref, qp_ref, gp_ref,
    or_ref, op_ref, dqr_ref, dqp_ref, fs_ref, dkv_ref,
    k_s, v_s, kt_s, vt_s, s_s, d_s, acck, accv,
):
    heads = qr_ref.shape[1] // D
    resp = qr_ref.shape[0]
    keys = k_s.shape[0]
    parts = dkv_ref.shape[0]
    slots = s_s.shape[0]
    k_s[...] = kv_ref[:, 0].reshape(keys, D)
    v_s[...] = kv_ref[:, 1].reshape(keys, D)
    kt_s[...] = k_s[...].T
    vt_s[...] = v_s[...].T
    first = first_ref[0]
    ahead = lax.broadcasted_iota(jnp.int32, (CHUNK, 128), 0) - lax.broadcasted_iota(
        jnp.int32, (CHUNK, 128), 1
    )
    held = {}

    def load(a, b, h):
        c = slice(h * D, (h + 1) * D)
        return jnp.concatenate([a[:, c], b[:, c]], 0)

    def scores(h, k0):
        if k0 == 0:
            held[h] = {"q": load(qr_ref, qp_ref, h), "g": load(gr_ref, gp_ref, h)}
        d = held[h]
        at = slice(k0, k0 + CHUNK)
        s = mm(k_s[at, :], d["q"], NT)
        s = jnp.concatenate([s[:, :resp], jnp.where(ahead <= first - k0, s[:, resp:], MASKED)], 1)
        s_s[h % slots, at, :] = s
        peak = fold(s, jnp.max)
        d["m"] = jnp.maximum(d["m"], peak) if k0 else peak
        d_s[h % slots, at, :] = mm(v_s[at, :], d["g"], NT)

    def raised(h, k0):
        d = held[h]
        if k0 == 0:
            m = jnp.max(d["m"], 0, keepdims=True)
            peak = stat_ref[h, 0:1]
            both = jnp.maximum(m[:, :resp], peak)
            d["f"] = jnp.exp2((peak - both) * SCALE2)
            d["m"] = jnp.concatenate([both, m[:, resp:]], 1) * SCALE2
        at = slice(k0, k0 + CHUNK)
        p = jnp.exp2(s_s[h % slots, at, :] * SCALE2 - d["m"])
        s_s[h % slots, at, :] = p
        total = fold(p, jnp.sum)
        mix = fold(p * d_s[h % slots, at, :], jnp.sum)
        d["l"] = d["l"] + total if k0 else total
        d["t"] = d["t"] + mix if k0 else mix

    def products(h, k0):
        d = held[h]
        if k0 == 0:
            f = d["f"]
            l = jnp.sum(d["l"], 0, keepdims=True)
            t = jnp.sum(d["t"], 0, keepdims=True)
            l = jnp.concatenate([l[:, :resp] + f * stat_ref[h, 1:2], l[:, resp:]], 1)
            t = jnp.concatenate([t[:, :resp] + f * stat_ref[h, 2:3], t[:, resp:]], 1)
            d["inv"] = 1.0 / l
            d["delta"] = t * d["inv"]
            fs_ref[h, 0:1] = f * d["inv"][:, :resp]
            fs_ref[h, 1:2] = d["delta"][:, :resp]
        at = slice(k0, k0 + CHUNK)
        w = s_s[h % slots, at, :] * d["inv"]
        ds = (w * (d_s[h % slots, at, :] - d["delta"])).astype(BF)
        w = w.astype(BF)
        o = mm(vt_s[:, at], w, NN)
        dq = mm(kt_s[:, at], ds, NN)
        d["o"] = d["o"] + o if k0 else o
        d["dq"] = d["dq"] + dq if k0 else dq
        dv = mm(w, d["g"], NN)
        dk = mm(ds, d["q"], NN)
        accv[at, :] = accv[at, :] + dv if h else dv
        acck[at, :] = acck[at, :] + dk if h else dk
        if k0 + CHUNK == keys:
            c = slice(h * D, (h + 1) * D)
            o = d["o"].T
            dq = d["dq"].T * SCALE
            or_ref[:, c] = o[:resp]
            op_ref[:, c] = o[resp:].astype(BF)
            dqr_ref[:, c] = dq[:resp]
            dqp_ref[:, c] = dq[resp:].astype(BF)
            del held[h]

    for i in range(heads + 2):
        for k0 in range(0, keys, CHUNK):
            for late, stage in enumerate((scores, raised, products)):
                if 0 <= i - late < heads:
                    stage(i - late, k0)
    dkv_ref[:, 0] = (acck[...] * SCALE).astype(BF).reshape(parts, keys // parts, D)
    dkv_ref[:, 1] = accv[...].astype(BF).reshape(parts, keys // parts, D)


def shape(*dims, dtype=BF):
    return jax.ShapeDtypeStruct(dims, dtype)


def call(body, outs, operands, flops, scratch=(), scalars=0):
    vmem = pl.BlockSpec(memory_space=pltpu.VMEM)
    return pl.pallas_call(
        body,
        in_specs=[pl.BlockSpec(memory_space=pltpu.SMEM)] * scalars + [vmem] * (len(operands) - scalars),
        out_specs=[vmem] * len(outs),
        out_shape=outs,
        scratch_shapes=scratch,
        compiler_params=pltpu.CompilerParams(vmem_limit_bytes=48 * 2**20),
        cost_estimate=pl.CostEstimate(flops=flops, bytes_accessed=4 * 2**20, transcendentals=0),
        name=body.__name__,
    )(*operands)


def local(prompt_q, prefix_kv, resp_q, resp_kv, resp_segs, grad_prompt_out, grad_resp_out):
    groups = lax.axis_size("group")
    tensors = lax.axis_size("tensor")
    group_rank = lax.axis_index("group")
    rows = prefix_kv.shape[1]
    resp_dev = resp_q.shape[0]
    prompt_dev = prompt_q.shape[0]
    keys = rows * groups * tensors
    both = ("group", "tensor")

    by_head = prefix_kv.reshape(2, rows, tensors, D).transpose(2, 0, 1, 3)
    to_send = jnp.broadcast_to(by_head[None], (groups,) + by_head.shape).reshape(-1, 2, rows, D)
    kv = lax.all_to_all(to_send, both, 0, 0, tiled=True)
    prior = lax.ppermute(
        resp_kv[:, resp_dev - BACK :], "group", [(i, i + 1) for i in range(groups - 1)]
    )
    lkv = jnp.concatenate([prior, resp_kv], 1)

    segs = jnp.concatenate([jnp.full((BACK,), -1, jnp.int32), resp_segs])
    segs = lax.dynamic_slice_in_dim(segs, group_rank * resp_dev, BACK + resp_dev)
    places = jnp.arange(BACK + resp_dev, dtype=jnp.int32)

    def local_bias(k0, k1, q0, q1):
        same = segs[k0:k1, None] == segs[None, q0:q1]
        return jnp.where(same & (places[k0:k1, None] <= places[None, q0:q1]), 0.0, MASKED).astype(F)

    bias_l = jnp.stack([local_bias(0, 192, 64, 192), local_bias(128, 320, 192, 320)])
    first = (group_rank * prompt_dev).astype(jnp.int32).reshape(1)
    width = resp_q.shape[1]
    heads = width // D
    rows_all = resp_dev + prompt_dev
    work = 2 * D * heads
    p_loc, stats = call(
        local_forward,
        [shape(2, 192, heads * 128), shape(heads, 8, resp_dev, dtype=F)],
        (lkv, bias_l, resp_q, grad_resp_out),
        work * 2 * 192 * resp_dev,
    )

    wide = (resp_dev, width)
    vm = pltpu.VMEM
    out1, prompt_out, dq1, grad_prompt_q, factors, terms = call(
        prefix_attention,
        [
            shape(*wide, dtype=F), shape(prompt_dev, width), shape(*wide, dtype=F), shape(prompt_dev, width),
            shape(heads, 8, resp_dev, dtype=F), shape(*kv.shape),
        ],
        (first, kv, stats, resp_q, grad_resp_out, prompt_q, grad_prompt_out),
        work * 6 * keys * rows_all,
        [vm((keys, D), BF), vm((keys, D), BF), vm((D, keys), BF), vm((D, keys), BF)]
        + [vm((3, keys, rows_all), F)] * 2
        + [vm((keys, D), F)] * 2,
        1,
    )
    arrived = lax.all_to_all(terms, both, 0, 0, tiled=True)
    local_terms, resp_out, grad_resp_q = call(
        local_backward,
        [shape(2, BACK + resp_dev, D, dtype=F), shape(*wide), shape(*wide)],
        (lkv, p_loc, factors, resp_q, grad_resp_out, out1, dq1),
        work * 5 * 192 * resp_dev,
    )
    later = lax.ppermute(
        local_terms[:, :BACK].astype(BF), "group", [(i, i - 1) for i in range(1, groups)]
    )
    grad_resp_kv = jnp.concatenate(
        [local_terms[:, BACK:resp_dev], local_terms[:, resp_dev:] + later.astype(F)], 1
    ).astype(BF)
    summed = arrived.reshape(groups, tensors, 2, rows, D).astype(F).sum(0).astype(BF)
    grad_prefix_kv = summed.transpose(1, 2, 0, 3).reshape(2, rows, tensors * D)
    return (prompt_out, resp_out, grad_prompt_q, grad_resp_q, grad_prefix_kv, grad_resp_kv)


def solution(mesh):
    wide = P(("prompt", "group"), "tensor")
    cache = P(None, ("prompt", "group", "tensor"), None)
    packed = P(None, ("prompt", "group"), "tensor")
    return jax.shard_map(
        local,
        mesh=mesh,
        in_specs=(wide, cache, wide, packed, P("prompt"), wide, wide),
        out_specs=(wide, wide, wide, wide, cache, packed),
        check_vma=False,
    )
```

```python
import math

import jax
import jax.numpy as jnp
from jax import lax
from jax.experimental import pallas as pl
from jax.experimental.pallas import tpu as pltpu
from jax.sharding import Mesh
from jax.sharding import PartitionSpec as P

D = 128
BF = jnp.bfloat16
F = jnp.float32
SCALE = D**-0.5
SCALE2 = SCALE * math.log2(math.e)
MASKED = -1e30
GROUP = ("chip", "core")
BACK = 64
NT = (((1,), (1,)), ((), ()))
TN = (((0,), (0,)), ((), ()))
NN = (((1,), (0,)), ((), ()))
CHUNK = 1024
UNIT = 2


def mm(a, b, dims):
    return lax.dot_general(a, b, dims, preferred_element_type=F)


def fold(x, op):
    return op(x.reshape(x.shape[0] // 8, 8, x.shape[1]), 0)


def stack_heads(ref, rows):
    return jnp.concatenate([ref[rows, i : i + D] for i in range(0, ref.shape[1], D)], 0)


def spread(kv_ref, out_ref, buffer, sem):
    count = buffer.shape[0]
    for t in range(count):
        buffer[t] = kv_ref[:, :, t * D : (t + 1) * D]
    copies = [
        pltpu.make_async_copy(buffer, out_ref.at[i : i + count], sem.at[i // count])
        for i in range(0, out_ref.shape[0], count)
    ]
    for copy in copies:
        copy.start()
    for copy in copies:
        copy.wait()


def gathered_sum(in_ref, out_ref):
    count = out_ref.shape[2] // D
    for t in range(count):
        total = in_ref[t].astype(F)
        for i in range(t + count, in_ref.shape[0], count):
            total = total + in_ref[i].astype(F)
        out_ref[:, :, t * D : (t + 1) * D] = total.astype(BF)


def local_parts(segs_ref, prior_ref, kv_ref, q_ref, g_ref):
    half = q_ref.shape[0] // 2
    start = pl.multiple_of(lax.axis_index(GROUP) * 2 * half, 2 * half)
    before = segs_ref[:, pl.ds(pl.multiple_of(jnp.maximum(start - half, 0), half), half)]
    before = jnp.where(start > 0, before, -1)[:, half - BACK :]
    segs = jnp.concatenate([before, segs_ref[:, pl.ds(start, 2 * half)]], 1).astype(F)
    by_key = jnp.broadcast_to(segs, (half, segs.shape[1])).T
    for i in range(2):
        rows = slice(i * half, (i + 1) * half)
        span = slice(i * half, i * half + half + BACK)
        k = jnp.concatenate([prior_ref[0], kv_ref[0]], 0)[span]
        v = jnp.concatenate([prior_ref[1], kv_ref[1]], 0)[span]
        behind = lax.broadcasted_iota(jnp.int32, (half + BACK, half), 0) - lax.broadcasted_iota(
            jnp.int32, (half + BACK, half), 1
        )
        same = by_key[span] == segs[:, i * half + BACK : (i + 1) * half + BACK]
        bias = jnp.where(same & (behind <= BACK), 0.0, MASKED)
        q = stack_heads(q_ref, rows)
        g = stack_heads(g_ref, rows)
        s = mm(k, q, NT) + jnp.concatenate([bias] * (q_ref.shape[1] // D), 1)
        yield rows, k, v, q, g, s


def local_forward(segs_ref, prior_ref, kv_ref, q_ref, g_ref, stat_ref):
    heads = q_ref.shape[1] // D
    for rows, k, v, q, g, s in local_parts(segs_ref, prior_ref, kv_ref, q_ref, g_ref):
        m = jnp.max(s, 0, keepdims=True)
        p = jnp.exp2((s - m) * SCALE2)
        total = jnp.sum(p, 0, keepdims=True)
        mix = jnp.sum(p * mm(v, g, NT), 0, keepdims=True)
        for h in range(heads):
            c = slice(h * 128, (h + 1) * 128)
            stat_ref[h, 0:1, rows] = m[:, c]
            stat_ref[h, 1:2, rows] = total[:, c]
            stat_ref[h, 2:3, rows] = mix[:, c]


def local_backward(
    segs_ref, prior_ref, kv_ref, q_ref, g_ref, stat_ref, fs_ref, o1_ref, dq1_ref,
    back_ref, rest_ref, dkv_ref, o_ref, dq_ref,
):
    heads = q_ref.shape[1] // D
    terms = []
    for rows, k, v, q, g, s in local_parts(segs_ref, prior_ref, kv_ref, q_ref, g_ref):
        m = jnp.concatenate([stat_ref[h, 0:1, rows] for h in range(heads)], 1)
        f = jnp.concatenate([fs_ref[h, 0:1, rows] for h in range(heads)], 1)
        delta = jnp.concatenate([fs_ref[h, 1:2, rows] for h in range(heads)], 1)
        wf = jnp.exp2((s - m) * SCALE2) * f
        w = wf.astype(BF)
        ds = (wf * (mm(v, g, NT) - delta)).astype(BF)
        terms.append((mm(ds, q, NN) * SCALE, mm(w, g, NN)))
        o = mm(w, v, TN)
        dq = mm(ds, k, TN) * SCALE
        for h in range(heads):
            c = slice(h * D, (h + 1) * D)
            r = slice(h * 128, (h + 1) * 128)
            o_ref[rows, c] = (o[r] + o1_ref[rows, c].astype(F)).astype(BF)
            dq_ref[rows, c] = (dq[r] + dq1_ref[rows, c].astype(F)).astype(BF)
    for x in range(2):
        a, b = terms[0][x], terms[1][x]
        back_ref[x] = a[0:64].astype(BF)
        dkv_ref[x, 0:64] = a[64:128].astype(BF)
        dkv_ref[x, 64:128] = (a[128:192] + b[0:64]).astype(BF)
        dkv_ref[x, 128:192] = b[64:128].astype(BF)
        dkv_ref[x, 192:256] = b[128:192].astype(BF)
        rest_ref[x] = b[128:192]


def prefix_attention(
    own_ref, other_ref, stat_ref, qr_ref, gr_ref, qp_ref, gp_ref,
    or_ref, op_ref, dqr_ref, dqp_ref, fs_ref, terms_ref,
    k_s, v_s, kt_s, vt_s, s_s, d_s, acck, accv,
):
    heads = qr_ref.shape[1] // D
    keys = k_s.shape[0]
    slots = s_s.shape[0]
    each = keys // 8
    core = lax.axis_index("core")
    for x in range(4):
        for ref, c in ((own_ref, core), (other_ref, 1 - core)):
            at = pl.ds(pl.multiple_of((2 * x + c) * each, each), each)
            k_s[at, :] = ref[4 * x : 4 * x + 4, 0].reshape(each, D)
            v_s[at, :] = ref[4 * x : 4 * x + 4, 1].reshape(each, D)
    kt_s[...] = k_s[...].T
    vt_s[...] = v_s[...].T
    first = lax.axis_index(GROUP) * qp_ref.shape[0]
    ahead = lax.broadcasted_iota(jnp.int32, (CHUNK, 128), 0) - lax.broadcasted_iota(
        jnp.int32, (CHUNK, 128), 1
    )
    blocks = [(h, slice(i * 128, i * 128 + 128)) for h in range(heads) for i in range(2)]
    blocks += [(h, None) for h in range(heads)]
    units = [blocks[i : i + UNIT] for i in range(0, len(blocks), UNIT)]
    held = {}

    def load(resp, prompt, unit):
        c = lambda h: slice(h * D, (h + 1) * D)
        return jnp.concatenate([prompt[:, c(h)] if r is None else resp[r, c(h)] for h, r in unit], 0)

    def by_block(unit, x, near):
        parts = []
        for i, (h, r) in enumerate(unit):
            part = x[:, i * 128 : i * 128 + 128]
            parts.append(part if r is None else near(h, r, part))
        return jnp.concatenate(parts, 1)

    def scores(u, k0):
        unit = units[u]
        if k0 == 0:
            held[u] = {"q": load(qr_ref, qp_ref, unit), "g": load(gr_ref, gp_ref, unit)}
        d = held[u]
        at = slice(k0, k0 + CHUNK)
        s = mm(k_s[at, :], d["q"], NT)
        if unit[-1][1] is None:
            cut = [s[:, i * 128 : i * 128 + 128] for i in range(len(unit))]
            seen = ahead <= first - k0
            cut = [jnp.where(seen, x, MASKED) if r is None else x for x, (h, r) in zip(cut, unit)]
            s = jnp.concatenate(cut, 1)
        cols = slice(0, len(unit) * 128)
        s_s[u % slots, at, cols] = s
        peak = fold(s, jnp.max)
        d["m"] = jnp.maximum(d["m"], peak) if k0 else peak
        d_s[u % slots, at, cols] = mm(v_s[at, :], d["g"], NT)

    def raised(u, k0):
        unit = units[u]
        d = held[u]
        cols = slice(0, len(unit) * 128)
        if k0 == 0:
            m = jnp.max(d["m"], 0, keepdims=True)
            d["m"] = by_block(unit, m, lambda h, r, x: jnp.maximum(x, stat_ref[h, 0:1, r]))
            peak = by_block(unit, d["m"], lambda h, r, x: stat_ref[h, 0:1, r])
            d["f"] = jnp.exp2((peak - d["m"]) * SCALE2)
            d["m"] = d["m"] * SCALE2
        at = slice(k0, k0 + CHUNK)
        p = jnp.exp2(s_s[u % slots, at, cols] * SCALE2 - d["m"])
        s_s[u % slots, at, cols] = p
        total = fold(p, jnp.sum)
        mix = fold(p * d_s[u % slots, at, cols], jnp.sum)
        d["l"] = d["l"] + total if k0 else total
        d["t"] = d["t"] + mix if k0 else mix

    def products(u, k0):
        unit = units[u]
        d = held[u]
        cols = slice(0, len(unit) * 128)
        if k0 == 0:
            f = d["f"]
            l = jnp.sum(d["l"], 0, keepdims=True)
            t = jnp.sum(d["t"], 0, keepdims=True)
            l = l + f * by_block(unit, jnp.zeros_like(l), lambda h, r, x: stat_ref[h, 1:2, r])
            t = t + f * by_block(unit, jnp.zeros_like(t), lambda h, r, x: stat_ref[h, 2:3, r])
            d["inv"] = 1.0 / l
            d["delta"] = t * d["inv"]
            f = f * d["inv"]
            for i, (h, r) in enumerate(unit):
                if r is not None:
                    fs_ref[h, 0:1, r] = f[:, i * 128 : i * 128 + 128]
                    fs_ref[h, 1:2, r] = d["delta"][:, i * 128 : i * 128 + 128]
        at = slice(k0, k0 + CHUNK)
        w = s_s[u % slots, at, cols] * d["inv"]
        ds = (w * (d_s[u % slots, at, cols] - d["delta"])).astype(BF)
        w = w.astype(BF)
        o = mm(vt_s[:, at], w, NN)
        dq = mm(kt_s[:, at], ds, NN)
        d["o"] = d["o"] + o if k0 else o
        d["dq"] = d["dq"] + dq if k0 else dq
        dv = mm(w, d["g"], NN)
        dk = mm(ds, d["q"], NN)
        accv[at, :] = accv[at, :] + dv if u else dv
        acck[at, :] = acck[at, :] + dk if u else dk
        if k0 + CHUNK == keys:
            o = d["o"].T
            dq = d["dq"].T * SCALE
            for i, (h, r) in enumerate(unit):
                c = slice(h * D, (h + 1) * D)
                a = slice(i * 128, i * 128 + 128)
                if r is None:
                    op_ref[:, c] = o[a].astype(BF)
                    dqp_ref[:, c] = dq[a].astype(BF)
                else:
                    or_ref[r, c] = o[a].astype(BF)
                    dqr_ref[r, c] = dq[a].astype(BF)
            del held[u]

    for i in range(len(units) + 2):
        for k0 in range(0, keys, CHUNK):
            for late, stage in enumerate((scores, raised, products)):
                if 0 <= i - late < len(units):
                    stage(i - late, k0)
    terms_ref[:, 0] = (acck[...] * SCALE).astype(BF).reshape(-1, keys // terms_ref.shape[0], D)
    terms_ref[:, 1] = accv[...].astype(BF).reshape(-1, keys // terms_ref.shape[0], D)


def shape(*dims, dtype=BF):
    return jax.ShapeDtypeStruct(dims, dtype)


def call(body, outs, operands, flops, scratch=(), grant=16):
    vmem = pl.BlockSpec(memory_space=pltpu.VMEM)
    return pl.pallas_call(
        body,
        in_specs=[vmem] * len(operands),
        out_specs=[vmem] * len(outs),
        out_shape=outs,
        scratch_shapes=scratch,
        compiler_params=pltpu.CompilerParams(vmem_limit_bytes=grant * 2**20),
        cost_estimate=pl.CostEstimate(flops=flops, bytes_accessed=4 * 2**20, transcendentals=0),
        name=body.__name__,
    )(*operands)


def local(prompt_q, prefix_kv, resp_q, resp_kv, resp_segs, grad_prompt_out, grad_resp_out):
    groups = lax.axis_size(GROUP)
    tensors = lax.axis_size("tensor")
    group_rank = lax.axis_index(GROUP)
    rows = prefix_kv.shape[1]
    resp_dev = resp_q.shape[0]
    prompt_dev = prompt_q.shape[0]
    keys = rows * groups * tensors
    both = GROUP + ("tensor",)

    chips = groups // 2
    vm = pltpu.VMEM
    to_send = pl.pallas_call(
        spread,
        in_specs=[pl.BlockSpec(memory_space=vm)],
        out_specs=pl.BlockSpec(memory_space=pl.ANY),
        out_shape=shape(chips * tensors, 2, rows, D),
        scratch_shapes=[vm((tensors, 2, rows, D), BF), pltpu.SemaphoreType.DMA((chips,))],
        cost_estimate=pl.CostEstimate(flops=0, bytes_accessed=2**18, transcendentals=0),
        name="spread",
    )(prefix_kv)
    to_send, held_kv = lax.optimization_barrier((to_send, resp_kv))
    tail = held_kv[:, resp_dev - BACK :]
    own = lax.all_to_all(to_send, ("chip", "tensor"), 0, 0, tiled=True)

    prior = lax.ppermute(tail, GROUP, [(i, i + 1) for i in range(groups - 1)])

    own, prior = lax.optimization_barrier((own, prior))
    other = lax.ppermute(own, "core", [(0, 1), (1, 0)])

    width = resp_q.shape[1]
    heads = width // D
    rows_all = resp_dev + prompt_dev
    work = 2 * D * heads
    near = (resp_segs.reshape(1, -1), prior, resp_kv, resp_q, grad_resp_out)
    (stats,) = call(local_forward, [shape(heads, 8, resp_dev, dtype=F)], near, work * 2 * 192 * resp_dev)
    wide = (resp_dev, width)
    out1, prompt_out, dq1, grad_prompt_q, factors, terms = call(
        prefix_attention,
        [
            shape(*wide), shape(prompt_dev, width), shape(*wide), shape(prompt_dev, width),
            shape(heads, 8, resp_dev, dtype=F), shape(groups * tensors, 2, rows, D),
        ],
        (own, other, stats, resp_q, grad_resp_out, prompt_q, grad_prompt_out),
        work * 6 * keys * rows_all,
        [vm((keys, D), BF), vm((keys, D), BF), vm((D, keys), BF), vm((D, keys), BF)]
        + [vm((3, keys, UNIT * 128), F)] * 2
        + [vm((keys, D), F)] * 2,
        24,
    )
    arrived = lax.all_to_all(terms, both, 0, 0, tiled=True)
    back, rest, grad_resp_kv, resp_out, grad_resp_q = call(
        local_backward,
        [shape(2, BACK, D), shape(2, BACK, D, dtype=F), shape(2, resp_dev, D), shape(*wide), shape(*wide)],
        near + (stats, factors, out1, dq1),
        work * 5 * 192 * resp_dev,
    )
    later = lax.ppermute(back, GROUP, [(i, i - 1) for i in range(1, groups)])
    grad_resp_kv = lax.dynamic_update_slice(
        grad_resp_kv, (rest + later.astype(F)).astype(BF), (0, resp_dev - BACK, 0)
    )
    (grad_prefix_kv,) = call(gathered_sum, [shape(2, rows, tensors * D)], (arrived,), 2**20)
    return (prompt_out, resp_out, grad_prompt_q, grad_resp_q, grad_prefix_kv, grad_resp_kv)


def solution(mesh):
    prompts, groups, tensors = mesh.devices.shape
    parts = Mesh(mesh.devices.reshape(prompts, groups // 2, 2, tensors), ("prompt",) + GROUP + ("tensor",))
    wide = P(("prompt",) + GROUP, "tensor")
    cache = P(None, ("prompt",) + GROUP + ("tensor",), None)
    packed = P(None, ("prompt",) + GROUP, "tensor")
    return jax.shard_map(
        local,
        mesh=parts,
        in_specs=(wide, cache, wide, packed, P("prompt"), wide, wide),
        out_specs=(wide, wide, wide, wide, cache, packed),
        check_vma=False,
    )
```

```python
import math

import jax
import jax.numpy as jnp
from jax import lax
from jax.experimental import pallas as pl
from jax.experimental.pallas import tpu as pltpu
from jax.sharding import Mesh
from jax.sharding import PartitionSpec as P

D = 128
BF = jnp.bfloat16
F = jnp.float32
SCALE = D**-0.5
SCALE2 = SCALE * math.log2(math.e)
MASKED = -1e30
GROUP = ("chip", "core")
BACK = 64
NT = (((1,), (1,)), ((), ()))
TN = (((0,), (0,)), ((), ()))
NN = (((1,), (0,)), ((), ()))
CHUNK = 1024
UNIT = 2


def mm(a, b, dims):
    return lax.dot_general(a, b, dims, preferred_element_type=F)


def fold(x, op):
    return op(x.reshape(x.shape[0] // 8, 8, x.shape[1]), 0)


def stack_heads(ref, rows):
    return jnp.concatenate([ref[rows, i : i + D] for i in range(0, ref.shape[1], D)], 0)


def spread(kv_ref, out_ref, buffer, sem):
    count = buffer.shape[0]
    for t in range(count):
        buffer[t] = kv_ref[:, :, t * D : (t + 1) * D]
    copies = [
        pltpu.make_async_copy(buffer, out_ref.at[i : i + count], sem.at[i // count])
        for i in range(0, out_ref.shape[0], count)
    ]
    for copy in copies:
        copy.start()
    for copy in copies:
        copy.wait()


def gathered_sum(in_ref, out_ref):
    count = out_ref.shape[2] // D
    for t in range(count):
        total = in_ref[t].astype(F)
        for i in range(t + count, in_ref.shape[0], count):
            total = total + in_ref[i].astype(F)
        out_ref[:, :, t * D : (t + 1) * D] = total.astype(BF)


def local_parts(segs_ref, lkv_ref, q_ref, g_ref):
    half = q_ref.shape[0] // 2
    start = pl.multiple_of(lax.axis_index(GROUP) * 2 * half, 2 * half)
    before = segs_ref[:, pl.ds(pl.multiple_of(jnp.maximum(start - half, 0), half), half)]
    before = jnp.where(start > 0, before, -1.0)[:, half - BACK :]
    segs = jnp.concatenate([before, segs_ref[:, pl.ds(start, 2 * half)]], 1)
    by_key = jnp.broadcast_to(segs, (half, segs.shape[1])).T
    for i in range(2):
        rows = slice(i * half, (i + 1) * half)
        span = slice(i * half, i * half + half + BACK)
        k = lkv_ref[0, span]
        v = lkv_ref[1, span]
        behind = lax.broadcasted_iota(jnp.int32, (half + BACK, half), 0) - lax.broadcasted_iota(
            jnp.int32, (half + BACK, half), 1
        )
        same = by_key[span] == segs[:, i * half + BACK : (i + 1) * half + BACK]
        bias = jnp.where(same & (behind <= BACK), 0.0, MASKED)
        q = stack_heads(q_ref, rows)
        g = stack_heads(g_ref, rows)
        s = mm(k, q, NT) + jnp.concatenate([bias] * (q_ref.shape[1] // D), 1)
        yield rows, k, v, q, g, s


def local_forward(segs_ref, lkv_ref, q_ref, g_ref, stat_ref):
    heads = q_ref.shape[1] // D
    for rows, k, v, q, g, s in local_parts(segs_ref, lkv_ref, q_ref, g_ref):
        m = jnp.max(s, 0, keepdims=True)
        p = jnp.exp2((s - m) * SCALE2)
        total = jnp.sum(p, 0, keepdims=True)
        mix = jnp.sum(p * mm(v, g, NT), 0, keepdims=True)
        for h in range(heads):
            c = slice(h * 128, (h + 1) * 128)
            stat_ref[h, 0:1, rows] = m[:, c]
            stat_ref[h, 1:2, rows] = total[:, c]
            stat_ref[h, 2:3, rows] = mix[:, c]


def local_backward(
    segs_ref, lkv_ref, q_ref, g_ref, stat_ref, fs_ref, o1_ref, dq1_ref,
    back_ref, rest_ref, dkv_ref, o_ref, dq_ref,
):
    heads = q_ref.shape[1] // D
    terms = []
    for rows, k, v, q, g, s in local_parts(segs_ref, lkv_ref, q_ref, g_ref):
        m = jnp.concatenate([stat_ref[h, 0:1, rows] for h in range(heads)], 1)
        f = jnp.concatenate([fs_ref[h, 0:1, rows] for h in range(heads)], 1)
        delta = jnp.concatenate([fs_ref[h, 1:2, rows] for h in range(heads)], 1)
        wf = jnp.exp2((s - m) * SCALE2) * f
        w = wf.astype(BF)
        ds = (wf * (mm(v, g, NT) - delta)).astype(BF)
        terms.append((mm(ds, q, NN) * SCALE, mm(w, g, NN)))
        o = mm(w, v, TN)
        dq = mm(ds, k, TN) * SCALE
        for h in range(heads):
            c = slice(h * D, (h + 1) * D)
            r = slice(h * 128, (h + 1) * 128)
            o_ref[rows, c] = (o[r] + o1_ref[rows, c].astype(F)).astype(BF)
            dq_ref[rows, c] = (dq[r] + dq1_ref[rows, c].astype(F)).astype(BF)
    for x in range(2):
        a, b = terms[0][x], terms[1][x]
        back_ref[x] = a[0:64].astype(BF)
        dkv_ref[x, 0:64] = a[64:128].astype(BF)
        dkv_ref[x, 64:128] = (a[128:192] + b[0:64]).astype(BF)
        dkv_ref[x, 128:192] = b[64:128].astype(BF)
        dkv_ref[x, 192:256] = b[128:192].astype(BF)
        rest_ref[x] = b[128:192]


def prefix_attention(
    own_ref, other_ref, stat_ref, qr_ref, gr_ref, qp_ref, gp_ref,
    or_ref, op_ref, dqr_ref, dqp_ref, fs_ref, terms_ref,
    k_s, v_s, kt_s, vt_s, s_s, d_s, acck, accv,
):
    heads = qr_ref.shape[1] // D
    keys = k_s.shape[0]
    slots = s_s.shape[0]
    each = keys // 8
    core = lax.axis_index("core")
    for x in range(4):
        for ref, c in ((own_ref, core), (other_ref, 1 - core)):
            at = pl.ds(pl.multiple_of((2 * x + c) * each, each), each)
            k_s[at, :] = ref[4 * x : 4 * x + 4, 0].reshape(each, D)
            v_s[at, :] = ref[4 * x : 4 * x + 4, 1].reshape(each, D)
    kt_s[...] = k_s[...].T
    vt_s[...] = v_s[...].T
    first = lax.axis_index(GROUP) * qp_ref.shape[0]
    ahead = lax.broadcasted_iota(jnp.int32, (CHUNK, 128), 0) - lax.broadcasted_iota(
        jnp.int32, (CHUNK, 128), 1
    )
    blocks = [(h, slice(i * 128, i * 128 + 128)) for h in range(heads) for i in range(2)]
    blocks += [(h, None) for h in range(heads)]
    units = [blocks[i : i + UNIT] for i in range(0, len(blocks), UNIT)]
    held = {}

    def load(resp, prompt, unit):
        c = lambda h: slice(h * D, (h + 1) * D)
        return jnp.concatenate([prompt[:, c(h)] if r is None else resp[r, c(h)] for h, r in unit], 0)

    def by_block(unit, x, near):
        parts = []
        for i, (h, r) in enumerate(unit):
            part = x[:, i * 128 : i * 128 + 128]
            parts.append(part if r is None else near(h, r, part))
        return jnp.concatenate(parts, 1)

    def scores(u, k0):
        unit = units[u]
        if k0 == 0:
            held[u] = {"q": load(qr_ref, qp_ref, unit), "g": load(gr_ref, gp_ref, unit)}
        d = held[u]
        at = slice(k0, k0 + CHUNK)
        s = mm(k_s[at, :], d["q"], NT)
        if unit[-1][1] is None:
            cut = [s[:, i * 128 : i * 128 + 128] for i in range(len(unit))]
            seen = ahead <= first - k0
            cut = [jnp.where(seen, x, MASKED) if r is None else x for x, (h, r) in zip(cut, unit)]
            s = jnp.concatenate(cut, 1)
        cols = slice(0, len(unit) * 128)
        s_s[u % slots, at, cols] = s
        peak = fold(s, jnp.max)
        d["m"] = jnp.maximum(d["m"], peak) if k0 else peak
        d_s[u % slots, at, cols] = mm(v_s[at, :], d["g"], NT)

    def raised(u, k0):
        unit = units[u]
        d = held[u]
        cols = slice(0, len(unit) * 128)
        if k0 == 0:
            m = jnp.max(d["m"], 0, keepdims=True)
            d["m"] = by_block(unit, m, lambda h, r, x: jnp.maximum(x, stat_ref[h, 0:1, r]))
            peak = by_block(unit, d["m"], lambda h, r, x: stat_ref[h, 0:1, r])
            d["f"] = jnp.exp2((peak - d["m"]) * SCALE2)
            d["m"] = d["m"] * SCALE2
        at = slice(k0, k0 + CHUNK)
        p = jnp.exp2(s_s[u % slots, at, cols] * SCALE2 - d["m"])
        s_s[u % slots, at, cols] = p
        total = fold(p, jnp.sum)
        mix = fold(p * d_s[u % slots, at, cols], jnp.sum)
        d["l"] = d["l"] + total if k0 else total
        d["t"] = d["t"] + mix if k0 else mix

    def products(u, k0):
        unit = units[u]
        d = held[u]
        cols = slice(0, len(unit) * 128)
        if k0 == 0:
            f = d["f"]
            l = jnp.sum(d["l"], 0, keepdims=True)
            t = jnp.sum(d["t"], 0, keepdims=True)
            l = l + f * by_block(unit, jnp.zeros_like(l), lambda h, r, x: stat_ref[h, 1:2, r])
            t = t + f * by_block(unit, jnp.zeros_like(t), lambda h, r, x: stat_ref[h, 2:3, r])
            d["inv"] = 1.0 / l
            d["delta"] = t * d["inv"]
            f = f * d["inv"]
            for i, (h, r) in enumerate(unit):
                if r is not None:
                    fs_ref[h, 0:1, r] = f[:, i * 128 : i * 128 + 128]
                    fs_ref[h, 1:2, r] = d["delta"][:, i * 128 : i * 128 + 128]
        at = slice(k0, k0 + CHUNK)
        w = s_s[u % slots, at, cols] * d["inv"]
        ds = (w * (d_s[u % slots, at, cols] - d["delta"])).astype(BF)
        w = w.astype(BF)
        o = mm(vt_s[:, at], w, NN)
        dq = mm(kt_s[:, at], ds, NN)
        d["o"] = d["o"] + o if k0 else o
        d["dq"] = d["dq"] + dq if k0 else dq
        dv = mm(w, d["g"], NN)
        dk = mm(ds, d["q"], NN)
        accv[at, :] = accv[at, :] + dv if u else dv
        acck[at, :] = acck[at, :] + dk if u else dk
        if k0 + CHUNK == keys:
            o = d["o"].T
            dq = d["dq"].T * SCALE
            for i, (h, r) in enumerate(unit):
                c = slice(h * D, (h + 1) * D)
                a = slice(i * 128, i * 128 + 128)
                if r is None:
                    op_ref[:, c] = o[a].astype(BF)
                    dqp_ref[:, c] = dq[a].astype(BF)
                else:
                    or_ref[r, c] = o[a].astype(BF)
                    dqr_ref[r, c] = dq[a].astype(BF)
            del held[u]

    for i in range(len(units) + 2):
        for k0 in range(0, keys, CHUNK):
            for late, stage in enumerate((scores, raised, products)):
                if 0 <= i - late < len(units):
                    stage(i - late, k0)
    terms_ref[:, 0] = (acck[...] * SCALE).astype(BF).reshape(-1, keys // terms_ref.shape[0], D)
    terms_ref[:, 1] = accv[...].astype(BF).reshape(-1, keys // terms_ref.shape[0], D)


def shape(*dims, dtype=BF):
    return jax.ShapeDtypeStruct(dims, dtype)


def call(body, outs, operands, flops, scratch=(), grant=16):
    vmem = pl.BlockSpec(memory_space=pltpu.VMEM)
    return pl.pallas_call(
        body,
        in_specs=[vmem] * len(operands),
        out_specs=[vmem] * len(outs),
        out_shape=outs,
        scratch_shapes=scratch,
        compiler_params=pltpu.CompilerParams(vmem_limit_bytes=grant * 2**20),
        cost_estimate=pl.CostEstimate(flops=flops, bytes_accessed=4 * 2**20, transcendentals=0),
        name=body.__name__,
    )(*operands)


def local(prompt_q, prefix_kv, resp_q, resp_kv, resp_segs, grad_prompt_out, grad_resp_out):
    groups = lax.axis_size(GROUP)
    tensors = lax.axis_size("tensor")
    group_rank = lax.axis_index(GROUP)
    rows = prefix_kv.shape[1]
    resp_dev = resp_q.shape[0]
    prompt_dev = prompt_q.shape[0]
    keys = rows * groups * tensors
    both = GROUP + ("tensor",)

    chips = groups // 2
    vm = pltpu.VMEM
    to_send = pl.pallas_call(
        spread,
        in_specs=[pl.BlockSpec(memory_space=vm)],
        out_specs=pl.BlockSpec(memory_space=pl.ANY),
        out_shape=shape(chips * tensors, 2, rows, D),
        scratch_shapes=[vm((tensors, 2, rows, D), BF), pltpu.SemaphoreType.DMA((chips,))],
        cost_estimate=pl.CostEstimate(flops=0, bytes_accessed=2**18, transcendentals=0),
        name="spread",
    )(prefix_kv)
    to_send, held_kv = lax.optimization_barrier((to_send, resp_kv))
    tail = held_kv[:, resp_dev - BACK :]
    own = lax.all_to_all(to_send, ("chip", "tensor"), 0, 0, tiled=True)

    prior = lax.ppermute(tail, GROUP, [(i, i + 1) for i in range(groups - 1)])

    lkv = jnp.concatenate([prior, resp_kv], 1)
    segs = resp_segs.astype(F).reshape(1, -1)
    own, lkv, segs = lax.optimization_barrier((own, lkv, segs))
    other = lax.ppermute(own, "core", [(0, 1), (1, 0)])

    width = resp_q.shape[1]
    heads = width // D
    rows_all = resp_dev + prompt_dev
    work = 2 * D * heads
    near = (segs, lkv, resp_q, grad_resp_out)
    (stats,) = call(local_forward, [shape(heads, 8, resp_dev, dtype=F)], near, work * 2 * 192 * resp_dev)
    wide = (resp_dev, width)
    out1, prompt_out, dq1, grad_prompt_q, factors, terms = call(
        prefix_attention,
        [
            shape(*wide), shape(prompt_dev, width), shape(*wide), shape(prompt_dev, width),
            shape(heads, 8, resp_dev, dtype=F), shape(groups * tensors, 2, rows, D),
        ],
        (own, other, stats, resp_q, grad_resp_out, prompt_q, grad_prompt_out),
        work * 6 * keys * rows_all,
        [vm((keys, D), BF), vm((keys, D), BF), vm((D, keys), BF), vm((D, keys), BF)]
        + [vm((3, keys, UNIT * 128), F)] * 2
        + [vm((keys, D), F)] * 2,
        24,
    )
    arrived = lax.all_to_all(terms, both, 0, 0, tiled=True)
    back, rest, grad_resp_kv, resp_out, grad_resp_q = call(
        local_backward,
        [shape(2, BACK, D), shape(2, BACK, D, dtype=F), shape(2, resp_dev, D), shape(*wide), shape(*wide)],
        near + (stats, factors, out1, dq1),
        work * 5 * 192 * resp_dev,
    )
    later = lax.ppermute(back, GROUP, [(i, i - 1) for i in range(1, groups)])
    grad_resp_kv = lax.dynamic_update_slice(
        grad_resp_kv, (rest + later.astype(F)).astype(BF), (0, resp_dev - BACK, 0)
    )
    (grad_prefix_kv,) = call(gathered_sum, [shape(2, rows, tensors * D)], (arrived,), 2**20)
    return (prompt_out, resp_out, grad_prompt_q, grad_resp_q, grad_prefix_kv, grad_resp_kv)


def solution(mesh):
    prompts, groups, tensors = mesh.devices.shape
    parts = Mesh(mesh.devices.reshape(prompts, groups // 2, 2, tensors), ("prompt",) + GROUP + ("tensor",))
    wide = P(("prompt",) + GROUP, "tensor")
    cache = P(None, ("prompt",) + GROUP + ("tensor",), None)
    packed = P(None, ("prompt",) + GROUP, "tensor")
    return jax.shard_map(
        local,
        mesh=parts,
        in_specs=(wide, cache, wide, packed, P("prompt"), wide, wide),
        out_specs=(wide, wide, wide, wide, cache, packed),
        check_vma=False,
    )
```

```python
import math

import jax
import jax.numpy as jnp
from jax import lax
from jax.experimental import pallas as pl
from jax.experimental.pallas import tpu as pltpu
from jax.sharding import Mesh
from jax.sharding import PartitionSpec as P

D = 128
BF = jnp.bfloat16
F = jnp.float32
SCALE = D**-0.5
SCALE2 = SCALE * math.log2(math.e)
MASKED = -1e30
GROUP = ("chip", "core")
BACK = 64
NT = (((1,), (1,)), ((), ()))
TN = (((0,), (0,)), ((), ()))
NN = (((1,), (0,)), ((), ()))
CHUNK = 1024
UNIT = 2


def mm(a, b, dims):
    return lax.dot_general(a, b, dims, preferred_element_type=F)


def fold(x, op):
    return op(x.reshape(x.shape[0] // 8, 8, x.shape[1]), 0)


def stack_heads(ref, rows):
    return jnp.concatenate([ref[rows, i : i + D] for i in range(0, ref.shape[1], D)], 0)


def spread(kv_ref, out_ref, buffer, sem):
    count = buffer.shape[0]
    for t in range(count):
        buffer[t] = kv_ref[:, :, t * D : (t + 1) * D]
    copies = [
        pltpu.make_async_copy(buffer, out_ref.at[i : i + count], sem.at[i // count])
        for i in range(0, out_ref.shape[0], count)
    ]
    for copy in copies:
        copy.start()
    for copy in copies:
        copy.wait()


def gathered_sum(in_ref, out_ref):
    count = out_ref.shape[2] // D
    for t in range(count):
        total = in_ref[t].astype(F)
        for i in range(t + count, in_ref.shape[0], count):
            total = total + in_ref[i].astype(F)
        out_ref[:, :, t * D : (t + 1) * D] = total.astype(BF)


def local_parts(segs_ref, lkv_ref, q_ref, g_ref):
    half = q_ref.shape[0] // 2
    start = pl.multiple_of(lax.axis_index(GROUP) * 2 * half, 2 * half)
    before = segs_ref[:, pl.ds(pl.multiple_of(jnp.maximum(start - half, 0), half), half)]
    before = jnp.where(start > 0, before, -1.0)[:, half - BACK :]
    segs = jnp.concatenate([before, segs_ref[:, pl.ds(start, 2 * half)]], 1)
    by_key = jnp.broadcast_to(segs, (half, segs.shape[1])).T
    for i in range(2):
        rows = slice(i * half, (i + 1) * half)
        span = slice(i * half, i * half + half + BACK)
        k = lkv_ref[0, span]
        v = lkv_ref[1, span]
        behind = lax.broadcasted_iota(jnp.int32, (half + BACK, half), 0) - lax.broadcasted_iota(
            jnp.int32, (half + BACK, half), 1
        )
        same = by_key[span] == segs[:, i * half + BACK : (i + 1) * half + BACK]
        bias = jnp.where(same & (behind <= BACK), 0.0, MASKED)
        q = stack_heads(q_ref, rows)
        g = stack_heads(g_ref, rows)
        s = mm(k, q, NT) + jnp.concatenate([bias] * (q_ref.shape[1] // D), 1)
        yield rows, k, v, q, g, s


def local_forward(segs_ref, lkv_ref, q_ref, g_ref, stat_ref):
    heads = q_ref.shape[1] // D
    for rows, k, v, q, g, s in local_parts(segs_ref, lkv_ref, q_ref, g_ref):
        m = jnp.max(s, 0, keepdims=True) * SCALE2
        p = jnp.exp2(s * SCALE2 - m)
        total = jnp.sum(p, 0, keepdims=True)
        mix = jnp.sum(p * mm(v, g, NT), 0, keepdims=True)
        for h in range(heads):
            c = slice(h * 128, (h + 1) * 128)
            stat_ref[h, 0:1, rows] = m[:, c]
            stat_ref[h, 1:2, rows] = total[:, c]
            stat_ref[h, 2:3, rows] = mix[:, c]


def local_backward(
    segs_ref, lkv_ref, q_ref, g_ref, stat_ref, fs_ref, o1_ref, dq1_ref,
    back_ref, rest_ref, dkv_ref, o_ref, dq_ref,
):
    heads = q_ref.shape[1] // D
    terms = []
    for rows, k, v, q, g, s in local_parts(segs_ref, lkv_ref, q_ref, g_ref):
        m = jnp.concatenate([stat_ref[h, 0:1, rows] for h in range(heads)], 1)
        f = jnp.concatenate([fs_ref[h, 0:1, rows] for h in range(heads)], 1)
        delta = jnp.concatenate([fs_ref[h, 1:2, rows] for h in range(heads)], 1)
        wf = jnp.exp2(s * SCALE2 - m) * f
        w = wf.astype(BF)
        ds = (wf * (mm(v, g, NT) - delta)).astype(BF)
        terms.append((mm(ds, q, NN) * SCALE, mm(w, g, NN)))
        o = mm(w, v, TN)
        dq = mm(ds, k, TN) * SCALE
        for h in range(heads):
            c = slice(h * D, (h + 1) * D)
            r = slice(h * 128, (h + 1) * 128)
            o_ref[rows, c] = (o[r] + o1_ref[rows, c].astype(F)).astype(BF)
            dq_ref[rows, c] = (dq[r] + dq1_ref[rows, c].astype(F)).astype(BF)
    for x in range(2):
        a, b = terms[0][x], terms[1][x]
        back_ref[x] = a[0:64].astype(BF)
        dkv_ref[x, 0:64] = a[64:128].astype(BF)
        dkv_ref[x, 64:128] = (a[128:192] + b[0:64]).astype(BF)
        dkv_ref[x, 128:192] = b[64:128].astype(BF)
        dkv_ref[x, 192:256] = b[128:192].astype(BF)
        rest_ref[x] = b[128:192]


def prefix_attention(
    own_ref, other_ref, stat_ref, qr_ref, gr_ref, qp_ref, gp_ref,
    or_ref, op_ref, dqr_ref, dqp_ref, fs_ref, terms_ref,
    k_s, v_s, kk_s, kt_s, vt_s, s_s, d_s, acck, accv,
):
    heads = qr_ref.shape[1] // D
    keys = k_s.shape[0]
    slots = s_s.shape[0]
    each = keys // 8
    core = lax.axis_index("core")
    for x in range(4):
        for ref, c in ((own_ref, core), (other_ref, 1 - core)):
            at = pl.ds(pl.multiple_of((2 * x + c) * each, each), each)
            k_s[at, :] = ref[4 * x : 4 * x + 4, 0].reshape(each, D)
            v_s[at, :] = ref[4 * x : 4 * x + 4, 1].reshape(each, D)
    scaled = k_s[...].astype(F) * SCALE2
    high = scaled.astype(BF)
    kk_s[:, :D] = high
    kk_s[:, D:] = (scaled - high.astype(F)).astype(BF)
    kt_s[...] = k_s[...].T
    vt_s[...] = v_s[...].T
    first = lax.axis_index(GROUP) * qp_ref.shape[0]
    ahead = lax.broadcasted_iota(jnp.int32, (CHUNK, 128), 0) - lax.broadcasted_iota(
        jnp.int32, (CHUNK, 128), 1
    )
    blocks = [(h, slice(i * 128, i * 128 + 128)) for h in range(heads) for i in range(2)]
    blocks += [(h, None) for h in range(heads)]
    units = [blocks[i : i + UNIT] for i in range(0, len(blocks), UNIT)]
    held = {}

    def load(resp, prompt, unit):
        c = lambda h: slice(h * D, (h + 1) * D)
        return jnp.concatenate([prompt[:, c(h)] if r is None else resp[r, c(h)] for h, r in unit], 0)

    def by_block(unit, x, near):
        parts = []
        for i, (h, r) in enumerate(unit):
            part = x[:, i * 128 : i * 128 + 128]
            parts.append(part if r is None else near(h, r, part))
        return jnp.concatenate(parts, 1)

    def scores(u, k0):
        unit = units[u]
        if k0 == 0:
            held[u] = {"q": load(qr_ref, qp_ref, unit), "g": load(gr_ref, gp_ref, unit)}
        d = held[u]
        at = slice(k0, k0 + CHUNK)
        s = mm(kk_s[at, :], jnp.concatenate([d["q"], d["q"]], 1), NT)
        if unit[-1][1] is None:
            cut = [s[:, i * 128 : i * 128 + 128] for i in range(len(unit))]
            seen = ahead <= first - k0
            cut = [jnp.where(seen, x, MASKED) if r is None else x for x, (h, r) in zip(cut, unit)]
            s = jnp.concatenate(cut, 1)
        cols = slice(0, len(unit) * 128)
        s_s[u % slots, at, cols] = s
        peak = fold(s, jnp.max)
        d["m"] = jnp.maximum(d["m"], peak) if k0 else peak
        d_s[u % slots, at, cols] = mm(v_s[at, :], d["g"], NT)

    def raised(u, k0):
        unit = units[u]
        d = held[u]
        cols = slice(0, len(unit) * 128)
        if k0 == 0:
            m = jnp.max(d["m"], 0, keepdims=True)
            d["m"] = by_block(unit, m, lambda h, r, x: jnp.maximum(x, stat_ref[h, 0:1, r]))
            peak = by_block(unit, d["m"], lambda h, r, x: stat_ref[h, 0:1, r])
            d["f"] = jnp.exp2(peak - d["m"])
        at = slice(k0, k0 + CHUNK)
        p = jnp.exp2(s_s[u % slots, at, cols] - d["m"])
        s_s[u % slots, at, cols] = p
        total = fold(p, jnp.sum)
        mix = fold(p * d_s[u % slots, at, cols], jnp.sum)
        d["l"] = d["l"] + total if k0 else total
        d["t"] = d["t"] + mix if k0 else mix

    def products(u, k0):
        unit = units[u]
        d = held[u]
        cols = slice(0, len(unit) * 128)
        if k0 == 0:
            f = d["f"]
            l = jnp.sum(d["l"], 0, keepdims=True)
            t = jnp.sum(d["t"], 0, keepdims=True)
            l = l + f * by_block(unit, jnp.zeros_like(l), lambda h, r, x: stat_ref[h, 1:2, r])
            t = t + f * by_block(unit, jnp.zeros_like(t), lambda h, r, x: stat_ref[h, 2:3, r])
            d["inv"] = 1.0 / l
            d["delta"] = t * d["inv"]
            f = f * d["inv"]
            for i, (h, r) in enumerate(unit):
                if r is not None:
                    fs_ref[h, 0:1, r] = f[:, i * 128 : i * 128 + 128]
                    fs_ref[h, 1:2, r] = d["delta"][:, i * 128 : i * 128 + 128]
        at = slice(k0, k0 + CHUNK)
        w = s_s[u % slots, at, cols] * d["inv"]
        ds = (w * (d_s[u % slots, at, cols] - d["delta"])).astype(BF)
        w = w.astype(BF)
        o = mm(vt_s[:, at], w, NN)
        dq = mm(kt_s[:, at], ds, NN)
        d["o"] = d["o"] + o if k0 else o
        d["dq"] = d["dq"] + dq if k0 else dq
        dv = mm(w, d["g"], NN)
        dk = mm(ds, d["q"], NN)
        accv[at, :] = accv[at, :] + dv if u else dv
        acck[at, :] = acck[at, :] + dk if u else dk
        if k0 + CHUNK == keys:
            o = d["o"].T
            dq = d["dq"].T * SCALE
            for i, (h, r) in enumerate(unit):
                c = slice(h * D, (h + 1) * D)
                a = slice(i * 128, i * 128 + 128)
                if r is None:
                    op_ref[:, c] = o[a].astype(BF)
                    dqp_ref[:, c] = dq[a].astype(BF)
                else:
                    or_ref[r, c] = o[a].astype(BF)
                    dqr_ref[r, c] = dq[a].astype(BF)
            del held[u]

    for i in range(len(units) + 2):
        for k0 in range(0, keys, CHUNK):
            for late, stage in enumerate((scores, raised, products)):
                if 0 <= i - late < len(units):
                    stage(i - late, k0)
    terms_ref[:, 0] = (acck[...] * SCALE).astype(BF).reshape(-1, keys // terms_ref.shape[0], D)
    terms_ref[:, 1] = accv[...].astype(BF).reshape(-1, keys // terms_ref.shape[0], D)


def shape(*dims, dtype=BF):
    return jax.ShapeDtypeStruct(dims, dtype)


def call(body, outs, operands, flops, scratch=(), grant=16):
    vmem = pl.BlockSpec(memory_space=pltpu.VMEM)
    return pl.pallas_call(
        body,
        in_specs=[vmem] * len(operands),
        out_specs=[vmem] * len(outs),
        out_shape=outs,
        scratch_shapes=scratch,
        compiler_params=pltpu.CompilerParams(vmem_limit_bytes=grant * 2**20),
        cost_estimate=pl.CostEstimate(flops=flops, bytes_accessed=4 * 2**20, transcendentals=0),
        name=body.__name__,
    )(*operands)


def local(prompt_q, prefix_kv, resp_q, resp_kv, resp_segs, grad_prompt_out, grad_resp_out):
    groups = lax.axis_size(GROUP)
    tensors = lax.axis_size("tensor")
    group_rank = lax.axis_index(GROUP)
    rows = prefix_kv.shape[1]
    resp_dev = resp_q.shape[0]
    prompt_dev = prompt_q.shape[0]
    keys = rows * groups * tensors
    both = GROUP + ("tensor",)

    chips = groups // 2
    vm = pltpu.VMEM
    to_send = pl.pallas_call(
        spread,
        in_specs=[pl.BlockSpec(memory_space=vm)],
        out_specs=pl.BlockSpec(memory_space=pl.ANY),
        out_shape=shape(chips * tensors, 2, rows, D),
        scratch_shapes=[vm((tensors, 2, rows, D), BF), pltpu.SemaphoreType.DMA((chips,))],
        cost_estimate=pl.CostEstimate(flops=0, bytes_accessed=2**18, transcendentals=0),
        name="spread",
    )(prefix_kv)
    to_send, held_kv = lax.optimization_barrier((to_send, resp_kv))
    tail = held_kv[:, resp_dev - BACK :]
    own = lax.all_to_all(to_send, ("chip", "tensor"), 0, 0, tiled=True)

    prior = lax.ppermute(tail, GROUP, [(i, i + 1) for i in range(groups - 1)])

    lkv = jnp.concatenate([prior, resp_kv], 1)
    segs = resp_segs.astype(F).reshape(1, -1)
    own, lkv, segs = lax.optimization_barrier((own, lkv, segs))
    other = lax.ppermute(own, "core", [(0, 1), (1, 0)])

    width = resp_q.shape[1]
    heads = width // D
    rows_all = resp_dev + prompt_dev
    work = 2 * D * heads
    near = (segs, lkv, resp_q, grad_resp_out)
    (stats,) = call(local_forward, [shape(heads, 8, resp_dev, dtype=F)], near, work * 2 * 192 * resp_dev)
    wide = (resp_dev, width)
    out1, prompt_out, dq1, grad_prompt_q, factors, terms = call(
        prefix_attention,
        [
            shape(*wide), shape(prompt_dev, width), shape(*wide), shape(prompt_dev, width),
            shape(heads, 8, resp_dev, dtype=F), shape(groups * tensors, 2, rows, D),
        ],
        (own, other, stats, resp_q, grad_resp_out, prompt_q, grad_prompt_out),
        work * 6 * keys * rows_all,
        [vm((keys, D), BF), vm((keys, D), BF), vm((keys, 2 * D), BF), vm((D, keys), BF), vm((D, keys), BF)]
        + [vm((3, keys, UNIT * 128), F)] * 2
        + [vm((keys, D), F)] * 2,
        24,
    )
    arrived = lax.all_to_all(terms, both, 0, 0, tiled=True)
    back, rest, grad_resp_kv, resp_out, grad_resp_q = call(
        local_backward,
        [shape(2, BACK, D), shape(2, BACK, D, dtype=F), shape(2, resp_dev, D), shape(*wide), shape(*wide)],
        near + (stats, factors, out1, dq1),
        work * 5 * 192 * resp_dev,
    )
    later = lax.ppermute(back, GROUP, [(i, i - 1) for i in range(1, groups)])
    grad_resp_kv = lax.dynamic_update_slice(
        grad_resp_kv, (rest + later.astype(F)).astype(BF), (0, resp_dev - BACK, 0)
    )
    (grad_prefix_kv,) = call(gathered_sum, [shape(2, rows, tensors * D)], (arrived,), 2**20)
    return (prompt_out, resp_out, grad_prompt_q, grad_resp_q, grad_prefix_kv, grad_resp_kv)


def solution(mesh):
    prompts, groups, tensors = mesh.devices.shape
    parts = Mesh(mesh.devices.reshape(prompts, groups // 2, 2, tensors), ("prompt",) + GROUP + ("tensor",))
    wide = P(("prompt",) + GROUP, "tensor")
    cache = P(None, ("prompt",) + GROUP + ("tensor",), None)
    packed = P(None, ("prompt",) + GROUP, "tensor")
    return jax.shard_map(
        local,
        mesh=parts,
        in_specs=(wide, cache, wide, packed, P("prompt"), wide, wide),
        out_specs=(wide, wide, wide, wide, cache, packed),
        check_vma=False,
    )
```

```python
import math

import jax
import jax.numpy as jnp
from jax import lax
from jax.experimental import pallas as pl
from jax.experimental.pallas import tpu as pltpu
from jax.sharding import Mesh
from jax.sharding import PartitionSpec as P

D = 128
BF = jnp.bfloat16
F = jnp.float32
SCALE = D**-0.5
SCALE2 = SCALE * math.log2(math.e)
MASKED = -1e30
GROUP = ("chip", "core")
BACK = 64
NT = (((1,), (1,)), ((), ()))
TN = (((0,), (0,)), ((), ()))
NN = (((1,), (0,)), ((), ()))
CHUNK = 1024
UNIT = 2


def mm(a, b, dims):
    return lax.dot_general(a, b, dims, preferred_element_type=F)


def fold(x, op):
    return op(x.reshape(x.shape[0] // 8, 8, x.shape[1]), 0)


def stack_heads(ref, rows):
    return jnp.concatenate([ref[rows, i : i + D] for i in range(0, ref.shape[1], D)], 0)


def spread(kv_ref, out_ref, buffer, sem):
    count = buffer.shape[0]
    arrivals = [
        pltpu.make_async_copy(kv_ref.at[:, :, pl.ds(t * D, D)], buffer.at[t], sem.at[t]) for t in range(count)
    ]
    copies = [
        pltpu.make_async_copy(buffer, out_ref.at[pl.ds(i, count)], sem.at[count + i // count])
        for i in range(0, out_ref.shape[0], count)
    ]
    for group in (arrivals, copies):
        for copy in group:
            copy.start()
        for copy in group:
            copy.wait()


def gathered_sum(in_ref, out_ref):
    count = out_ref.shape[2] // D
    for t in range(count):
        total = in_ref[t].astype(F)
        for i in range(t + count, in_ref.shape[0], count):
            total = total + in_ref[i].astype(F)
        out_ref[:, :, t * D : (t + 1) * D] = total.astype(BF)


def local_parts(segs_ref, lkv_ref, q_ref, g_ref):
    half = q_ref.shape[0] // 2
    start = pl.multiple_of(lax.axis_index(GROUP) * 2 * half, 2 * half)
    before = segs_ref[:, pl.ds(pl.multiple_of(jnp.maximum(start - half, 0), half), half)]
    before = jnp.where(start > 0, before, -1.0)[:, half - BACK :]
    segs = jnp.concatenate([before, segs_ref[:, pl.ds(start, 2 * half)]], 1)
    by_key = jnp.broadcast_to(segs, (half, segs.shape[1])).T
    for i in range(2):
        rows = slice(i * half, (i + 1) * half)
        span = slice(i * half, i * half + half + BACK)
        k = lkv_ref[0, span]
        v = lkv_ref[1, span]
        behind = lax.broadcasted_iota(jnp.int32, (half + BACK, half), 0) - lax.broadcasted_iota(
            jnp.int32, (half + BACK, half), 1
        )
        same = by_key[span] == segs[:, i * half + BACK : (i + 1) * half + BACK]
        bias = jnp.where(same & (behind <= BACK), 0.0, MASKED)
        q = stack_heads(q_ref, rows)
        g = stack_heads(g_ref, rows)
        s = mm(k, q, NT) + jnp.concatenate([bias] * (q_ref.shape[1] // D), 1)
        yield rows, k, v, q, g, s


def local_forward(segs_ref, lkv_ref, q_ref, g_ref, stat_ref):
    heads = q_ref.shape[1] // D
    for rows, k, v, q, g, s in local_parts(segs_ref, lkv_ref, q_ref, g_ref):
        m = jnp.max(s, 0, keepdims=True) * SCALE2
        p = jnp.exp2(s * SCALE2 - m)
        total = jnp.sum(p, 0, keepdims=True)
        mix = jnp.sum(p * mm(v, g, NT), 0, keepdims=True)
        for h in range(heads):
            c = slice(h * 128, (h + 1) * 128)
            stat_ref[h, 0:1, rows] = m[:, c]
            stat_ref[h, 1:2, rows] = total[:, c]
            stat_ref[h, 2:3, rows] = mix[:, c]


def local_backward(
    segs_ref, lkv_ref, q_ref, g_ref, stat_ref, fs_ref, o1_ref, dq1_ref,
    back_ref, rest_ref, dkv_ref, o_ref, dq_ref,
):
    heads = q_ref.shape[1] // D
    terms = []
    for rows, k, v, q, g, s in local_parts(segs_ref, lkv_ref, q_ref, g_ref):
        m = jnp.concatenate([stat_ref[h, 0:1, rows] for h in range(heads)], 1)
        f = jnp.concatenate([fs_ref[h, 0:1, rows] for h in range(heads)], 1)
        delta = jnp.concatenate([fs_ref[h, 1:2, rows] for h in range(heads)], 1)
        wf = jnp.exp2(s * SCALE2 - m) * f
        w = wf.astype(BF)
        ds = (wf * (mm(v, g, NT) - delta)).astype(BF)
        terms.append((mm(ds, q, NN) * SCALE, mm(w, g, NN)))
        o = mm(w, v, TN)
        dq = mm(ds, k, TN) * SCALE
        for h in range(heads):
            c = slice(h * D, (h + 1) * D)
            r = slice(h * 128, (h + 1) * 128)
            o_ref[rows, c] = (o[r] + o1_ref[rows, c].astype(F)).astype(BF)
            dq_ref[rows, c] = (dq[r] + dq1_ref[rows, c].astype(F)).astype(BF)
    for x in range(2):
        a, b = terms[0][x], terms[1][x]
        back_ref[x] = a[0:64].astype(BF)
        dkv_ref[x, 0:64] = a[64:128].astype(BF)
        dkv_ref[x, 64:128] = (a[128:192] + b[0:64]).astype(BF)
        dkv_ref[x, 128:192] = b[64:128].astype(BF)
        dkv_ref[x, 192:256] = b[128:192].astype(BF)
        rest_ref[x] = b[128:192]


def prefix_attention(
    own_ref, other_ref, stat_ref, qr_ref, gr_ref, qp_ref, gp_ref,
    or_ref, op_ref, dqr_ref, dqp_ref, fs_ref, terms_ref,
    k_s, v_s, kk_s, kt_s, vt_s, s_s, d_s, acck, accv,
):
    heads = qr_ref.shape[1] // D
    keys = k_s.shape[0]
    slots = s_s.shape[0]
    each = keys // 8
    core = lax.axis_index("core")
    for x in range(4):
        for ref, c in ((own_ref, core), (other_ref, 1 - core)):
            at = pl.ds(pl.multiple_of((2 * x + c) * each, each), each)
            k_s[at, :] = ref[4 * x : 4 * x + 4, 0].reshape(each, D)
            v_s[at, :] = ref[4 * x : 4 * x + 4, 1].reshape(each, D)
    scaled = k_s[...].astype(F) * SCALE2
    high = scaled.astype(BF)
    kk_s[:, :D] = high
    kk_s[:, D:] = (scaled - high.astype(F)).astype(BF)
    kt_s[...] = k_s[...].T
    vt_s[...] = v_s[...].T
    first = lax.axis_index(GROUP) * qp_ref.shape[0]
    ahead = lax.broadcasted_iota(jnp.int32, (CHUNK, 128), 0) - lax.broadcasted_iota(
        jnp.int32, (CHUNK, 128), 1
    )
    blocks = [(h, slice(i * 128, i * 128 + 128)) for h in range(heads) for i in range(2)]
    blocks += [(h, None) for h in range(heads)]
    units = [blocks[i : i + UNIT] for i in range(0, len(blocks), UNIT)]
    held = {}

    def load(resp, prompt, unit):
        c = lambda h: slice(h * D, (h + 1) * D)
        return jnp.concatenate([prompt[:, c(h)] if r is None else resp[r, c(h)] for h, r in unit], 0)

    def by_block(unit, x, near):
        parts = []
        for i, (h, r) in enumerate(unit):
            part = x[:, i * 128 : i * 128 + 128]
            parts.append(part if r is None else near(h, r, part))
        return jnp.concatenate(parts, 1)

    def scores(u, k0):
        unit = units[u]
        if k0 == 0:
            held[u] = {"q": load(qr_ref, qp_ref, unit), "g": load(gr_ref, gp_ref, unit)}
        d = held[u]
        at = slice(k0, k0 + CHUNK)
        s = mm(kk_s[at, :], jnp.concatenate([d["q"], d["q"]], 1), NT)
        if unit[-1][1] is None:
            cut = [s[:, i * 128 : i * 128 + 128] for i in range(len(unit))]
            seen = ahead <= first - k0
            cut = [jnp.where(seen, x, MASKED) if r is None else x for x, (h, r) in zip(cut, unit)]
            s = jnp.concatenate(cut, 1)
        cols = slice(0, len(unit) * 128)
        s_s[u % slots, at, cols] = s
        peak = fold(s, jnp.max)
        d["m"] = jnp.maximum(d["m"], peak) if k0 else peak
        d_s[u % slots, at, cols] = mm(v_s[at, :], d["g"], NT)

    def raised(u, k0):
        unit = units[u]
        d = held[u]
        cols = slice(0, len(unit) * 128)
        if k0 == 0:
            m = jnp.max(d["m"], 0, keepdims=True)
            d["m"] = by_block(unit, m, lambda h, r, x: jnp.maximum(x, stat_ref[h, 0:1, r]))
            peak = by_block(unit, d["m"], lambda h, r, x: stat_ref[h, 0:1, r])
            d["f"] = jnp.exp2(peak - d["m"])
        at = slice(k0, k0 + CHUNK)
        p = jnp.exp2(s_s[u % slots, at, cols] - d["m"])
        s_s[u % slots, at, cols] = p
        total = fold(p, jnp.sum)
        mix = fold(p * d_s[u % slots, at, cols], jnp.sum)
        d["l"] = d["l"] + total if k0 else total
        d["t"] = d["t"] + mix if k0 else mix

    def products(u, k0):
        unit = units[u]
        d = held[u]
        cols = slice(0, len(unit) * 128)
        if k0 == 0:
            f = d["f"]
            l = jnp.sum(d["l"], 0, keepdims=True)
            t = jnp.sum(d["t"], 0, keepdims=True)
            l = l + f * by_block(unit, jnp.zeros_like(l), lambda h, r, x: stat_ref[h, 1:2, r])
            t = t + f * by_block(unit, jnp.zeros_like(t), lambda h, r, x: stat_ref[h, 2:3, r])
            d["inv"] = 1.0 / l
            d["delta"] = t * d["inv"]
            f = f * d["inv"]
            for i, (h, r) in enumerate(unit):
                if r is not None:
                    fs_ref[h, 0:1, r] = f[:, i * 128 : i * 128 + 128]
                    fs_ref[h, 1:2, r] = d["delta"][:, i * 128 : i * 128 + 128]
        at = slice(k0, k0 + CHUNK)
        w = s_s[u % slots, at, cols] * d["inv"]
        ds = (w * (d_s[u % slots, at, cols] - d["delta"])).astype(BF)
        w = w.astype(BF)
        o = mm(vt_s[:, at], w, NN)
        dq = mm(kt_s[:, at], ds, NN)
        d["o"] = d["o"] + o if k0 else o
        d["dq"] = d["dq"] + dq if k0 else dq
        dv = mm(w, d["g"], NN)
        dk = mm(ds, d["q"], NN)
        if u + 1 < len(units):
            accv[at, :] = accv[at, :] + dv if u else dv
            acck[at, :] = acck[at, :] + dk if u else dk
        else:
            each_block = keys // terms_ref.shape[0]
            to = slice(k0 // each_block, (k0 + CHUNK) // each_block)
            terms_ref[to, 0] = ((acck[at, :] + dk) * SCALE).astype(BF).reshape(-1, each_block, D)
            terms_ref[to, 1] = (accv[at, :] + dv).astype(BF).reshape(-1, each_block, D)
        if k0 + CHUNK == keys:
            o = d["o"].T
            dq = d["dq"].T * SCALE
            for i, (h, r) in enumerate(unit):
                c = slice(h * D, (h + 1) * D)
                a = slice(i * 128, i * 128 + 128)
                if r is None:
                    op_ref[:, c] = o[a].astype(BF)
                    dqp_ref[:, c] = dq[a].astype(BF)
                else:
                    or_ref[r, c] = o[a].astype(BF)
                    dqr_ref[r, c] = dq[a].astype(BF)
            del held[u]

    for i in range(len(units) + 2):
        for k0 in range(0, keys, CHUNK):
            for late, stage in enumerate((scores, raised, products)):
                if 0 <= i - late < len(units):
                    stage(i - late, k0)


def shape(*dims, dtype=BF):
    return jax.ShapeDtypeStruct(dims, dtype)


def call(body, outs, operands, flops, scratch=(), grant=16):
    vmem = pl.BlockSpec(memory_space=pltpu.VMEM)
    return pl.pallas_call(
        body,
        in_specs=[vmem] * len(operands),
        out_specs=[vmem] * len(outs),
        out_shape=outs,
        scratch_shapes=scratch,
        compiler_params=pltpu.CompilerParams(vmem_limit_bytes=grant * 2**20),
        cost_estimate=pl.CostEstimate(flops=flops, bytes_accessed=4 * 2**20, transcendentals=0),
        name=body.__name__,
    )(*operands)


def local(prompt_q, prefix_kv, resp_q, resp_kv, resp_segs, grad_prompt_out, grad_resp_out):
    groups = lax.axis_size(GROUP)
    tensors = lax.axis_size("tensor")
    group_rank = lax.axis_index(GROUP)
    rows = prefix_kv.shape[1]
    resp_dev = resp_q.shape[0]
    prompt_dev = prompt_q.shape[0]
    keys = rows * groups * tensors
    both = GROUP + ("tensor",)

    chips = groups // 2
    vm = pltpu.VMEM
    to_send = pl.pallas_call(
        spread,
        in_specs=[pl.BlockSpec(memory_space=pl.ANY)],
        out_specs=pl.BlockSpec(memory_space=pl.ANY),
        out_shape=shape(chips * tensors, 2, rows, D),
        scratch_shapes=[vm((tensors, 2, rows, D), BF), pltpu.SemaphoreType.DMA((tensors + chips,))],
        compiler_params=pltpu.CompilerParams(vmem_limit_bytes=60 * 2**20),
        cost_estimate=pl.CostEstimate(flops=0, bytes_accessed=2**18, transcendentals=0),
        name="spread",
    )(prefix_kv)
    to_send, held_kv = lax.optimization_barrier((to_send, resp_kv))
    tail = held_kv[:, resp_dev - BACK :]
    own = lax.all_to_all(to_send, ("chip", "tensor"), 0, 0, tiled=True)

    prior = lax.ppermute(tail, GROUP, [(i, i + 1) for i in range(groups - 1)])

    lkv = jnp.concatenate([prior, resp_kv], 1)
    segs = resp_segs.astype(F).reshape(1, -1)
    own, lkv, segs = lax.optimization_barrier((own, lkv, segs))
    other = lax.ppermute(own, "core", [(0, 1), (1, 0)])

    width = resp_q.shape[1]
    heads = width // D
    rows_all = resp_dev + prompt_dev
    work = 2 * D * heads
    near = (segs, lkv, resp_q, grad_resp_out)
    (stats,) = call(local_forward, [shape(heads, 8, resp_dev, dtype=F)], near, work * 2 * 192 * resp_dev)
    wide = (resp_dev, width)
    out1, prompt_out, dq1, grad_prompt_q, factors, terms = call(
        prefix_attention,
        [
            shape(*wide), shape(prompt_dev, width), shape(*wide), shape(prompt_dev, width),
            shape(heads, 8, resp_dev, dtype=F), shape(groups * tensors, 2, rows, D),
        ],
        (own, other, stats, resp_q, grad_resp_out, prompt_q, grad_prompt_out),
        work * 6 * keys * rows_all,
        [vm((keys, D), BF), vm((keys, D), BF), vm((keys, 2 * D), BF), vm((D, keys), BF), vm((D, keys), BF)]
        + [vm((3, keys, UNIT * 128), F)] * 2
        + [vm((keys, D), F)] * 2,
        24,
    )
    arrived = lax.all_to_all(terms, both, 0, 0, tiled=True)
    back, rest, grad_resp_kv, resp_out, grad_resp_q = call(
        local_backward,
        [shape(2, BACK, D), shape(2, BACK, D, dtype=F), shape(2, resp_dev, D), shape(*wide), shape(*wide)],
        near + (stats, factors, out1, dq1),
        work * 5 * 192 * resp_dev,
    )
    later = lax.ppermute(back, GROUP, [(i, i - 1) for i in range(1, groups)])
    grad_resp_kv = lax.dynamic_update_slice(
        grad_resp_kv, (rest + later.astype(F)).astype(BF), (0, resp_dev - BACK, 0)
    )
    (grad_prefix_kv,) = call(gathered_sum, [shape(2, rows, tensors * D)], (arrived,), 2**20)
    return (prompt_out, resp_out, grad_prompt_q, grad_resp_q, grad_prefix_kv, grad_resp_kv)


def solution(mesh):
    prompts, groups, tensors = mesh.devices.shape
    parts = Mesh(mesh.devices.reshape(prompts, groups // 2, 2, tensors), ("prompt",) + GROUP + ("tensor",))
    wide = P(("prompt",) + GROUP, "tensor")
    cache = P(None, ("prompt",) + GROUP + ("tensor",), None)
    packed = P(None, ("prompt",) + GROUP, "tensor")
    return jax.shard_map(
        local,
        mesh=parts,
        in_specs=(wide, cache, wide, packed, P("prompt"), wide, wide),
        out_specs=(wide, wide, wide, wide, cache, packed),
        check_vma=False,
    )
```
